32 devices in a mesh: ctx: 8 (over z, y), ch: 4 (over x, core).
Axes of the slice: x: 2, y: 2, z: 4, core: 2. Of those that a mesh axis runs over, the one named last changes fastest.
Arguments:
- outer_gate: bfloat16 [2048, 4096], P('ctx', 'ch'), may hold values from -6 to 6
- inner_gate: bfloat16 [2048, 4096], P('ctx', 'ch'), may hold values from -6 to 6
- values_in: bfloat16 [2048, 4096], P('ctx', 'ch'), may hold values from -6 to 6
- filters: float32 [2048, 4096], P('ctx', 'ch'), as said below
- skip_gain: float32 [4096], P('ch'), may hold values from 0.5 to 1.5
- w_out: bfloat16 [4096, 4096], P('ch', 'ctx'), may hold values from -0.125 to 0.125
Outputs:
- mixed: bfloat16 [2048, 4096], P('ctx', 'ch')
The draws below stay inside these ranges and needn't reach their ends.
Inputs may be any that keep to these rules, and one draw needn't show every extreme that they name: `filters`: finite values.
All inputs are finite; a program needn't handle non-finite values.
Results may differ from the reference program's by a relative error of at most 0.022.
Values may be sent and summed in bfloat16 or wider, within the bound.
No kernel may reach another device: no remote copies, remote signals or barrier semaphores. Data moves between devices by JAX's collectives and lax.ppermute only.
A program may use at most 128 MiB of HBM per device.

```python
import math
import jax
import jax.numpy as jnp

D = 4096
SEQ = 2048


def draw_filters(key, part):
    key_tau = jax.random.fold_in(key, 0)
    key_noise = jax.random.fold_in(key, 1)
    key_slow = jax.random.fold_in(key, 3)
    key_share = jax.random.fold_in(key, 4)
    key_far = jax.random.fold_in(key, 5)
    lags = jnp.arange(SEQ, dtype=jnp.float32)[:, None]
    log_tau = jax.random.uniform(key_tau, (D,), jnp.float32, math.log(30.0), math.log(4.0 * SEQ))
    noise = jax.random.normal(key_noise, (SEQ, D), jnp.float32)
    far_noise = jax.random.normal(key_far, (SEQ, D), jnp.float32)
    scale = jnp.ones((D,), jnp.float32)
    tau = jnp.exp(log_tau)
    slow_tau = jnp.exp(jax.random.uniform(key_slow, (D,), jnp.float32, math.log(2.0 * SEQ), math.log(8.0 * SEQ)))
    slow_share = jnp.exp(jax.random.uniform(key_share, (D,), jnp.float32, math.log(0.5), 0.0))
    amplitude = scale / jnp.sqrt(jnp.minimum(tau, float(SEQ)))
    slow_amplitude = slow_share / math.sqrt(float(SEQ))
    fast_mode = amplitude[None, :] * jnp.exp(-lags / tau[None, :]) * noise
    slow_mode = slow_amplitude[None, :] * jnp.exp(-lags / slow_tau[None, :]) * far_noise
    return (fast_mode + slow_mode).astype(jnp.float32)


def strengthened(drawn, own_key, source, target, blocks, factor):
    owner, partner = [(jnp.arange(drawn.shape[axis_at]) // (drawn.shape[axis_at] // blocks)).reshape([-1 if axis == axis_at else 1 for axis in range(drawn.ndim)]) for axis_at in (source, target)]
    chosen = jax.random.permutation(own_key, blocks)[partner]
    strong = (owner == chosen) | (owner == (partner + blocks // 2) % blocks)
    return jnp.where(strong, factor * drawn, drawn)


def block_levels(stream_key, shape, pieces, least, largest):
    def one(position, parts):
        heights = jax.random.uniform(jax.random.fold_in(jax.random.fold_in(stream_key, 6), position), (parts,), jnp.float32, least / len(pieces), largest / len(pieces))
        return jnp.repeat(jnp.exp(heights), shape[position] // parts).reshape((-1,) + (1,) * (len(shape) - position - 1))

    factor_of = one(*pieces[0])
    for cut in pieces[1:]:
        factor_of = factor_of * one(*cut)
    return factor_of


def bell_draw(rng, extent, scale, reach, cuts=(), kind=jnp.bfloat16):
    entries = scale * jax.random.normal(rng, extent, jnp.float32)
    if cuts:
        entries = entries * block_levels(rng, extent, cuts, -0.22, 0.18)
    return jnp.clip(entries, -reach, reach).astype(kind)


def bell_draw_with(stream_key, dims, deviation, limit, cuts, heavy, held_as=jnp.bfloat16):
    drawn = deviation * jax.random.normal(stream_key, dims, jnp.float32)
    if cuts:
        drawn = drawn * block_levels(stream_key, dims, cuts, -0.22, 0.18)
    return jnp.clip(strengthened(drawn, jax.random.fold_in(stream_key, 3), *heavy), -limit, limit).astype(held_as)


def setup_inputs(seed: int = 0) -> dict:
    key_of = jax.random.split(jax.random.key(seed), 7)
    return {
        "outer_gate": bell_draw(key_of[0], (SEQ, D), 1.0, 6.0, ((0, 8), (1, 4))),
        "inner_gate": bell_draw(key_of[1], (SEQ, D), 1.0, 6.0, ((0, 8), (1, 4))),
        "values_in": bell_draw(key_of[2], (SEQ, D), 1.0, 6.0, ((0, 8), (1, 4))),
        "filters": draw_filters(jax.random.fold_in(key_of[6], 71), 0),
        "skip_gain": jnp.clip(0.5 + 1.0 * jax.random.uniform(key_of[4], (D,), jnp.float32) ** block_levels(key_of[4], (D,), ((0, 4),), -0.2, 0.2), 0.5, 1.5),
        "w_out": bell_draw_with(key_of[5], (D, D), D ** -0.5, 0.125, ((0, 4), (1, 8)), (0, 1, 8, 2.0)),
    }


def reference(outer_gate, inner_gate, values_in, filters, skip_gain, w_out):
    gated = (inner_gate.astype(jnp.float32) * values_in.astype(jnp.float32)).astype(jnp.bfloat16)
    gated_f = gated.astype(jnp.float32)
    length = 2 * SEQ
    spec_in = jnp.fft.rfft(gated_f, n=length, axis=0)
    spec_filter = jnp.fft.rfft(filters, n=length, axis=0)
    conv = jnp.fft.irfft(spec_in * spec_filter, n=length, axis=0)[:SEQ]
    mix_in = (outer_gate.astype(jnp.float32) * (conv + skip_gain[None, :] * gated_f)).astype(jnp.bfloat16)
    return jnp.dot(mix_in, w_out, preferred_element_type=jnp.float32).astype(jnp.bfloat16)
```

```python
import functools
import math

import jax
import jax.numpy as jnp
import numpy as np
from jax import lax
from jax.experimental import pallas as pl
from jax.experimental.pallas import tpu as pltpu
from jax.sharding import PartitionSpec as P


def tables(block):
    freqs = np.arange(block, dtype=np.float64)[:, None] + 0.5
    window = np.arange(-block, block, dtype=np.float64)[None, :]
    angles = math.pi / block * freqs * window
    forward = np.concatenate([np.cos(angles), -np.sin(angles)], axis=0)
    places = angles[:, block:].T
    inverse = np.concatenate([np.cos(places), -np.sin(places)], axis=1) / block
    return forward.astype(jnp.bfloat16), inverse.astype(jnp.bfloat16)


def conv_kernel(gf_ref, outer_ref, skip_ref, fwd_ref, inv_ref, mix_ref, xs, gs, ys):
    n, _, block, chans = gf_ref.shape
    f32 = jnp.float32
    for k in range(n):
        xs[k] = jnp.dot(fwd_ref[:, block:], gf_ref[k, 0], preferred_element_type=f32)
        lag = jnp.dot(fwd_ref[:, block:], gf_ref[k, 1], preferred_element_type=f32)
        if k:
            lag += jnp.dot(fwd_ref[:, :block], gf_ref[k - 1, 1], preferred_element_type=f32)
        gs[k] = lag

    step = 8

    @pl.loop(0, block // step)
    def _(c):
        re = pl.ds(pl.multiple_of(c * step, step), step)
        im = pl.ds(pl.multiple_of(block + c * step, step), step)
        xr = [xs[k, re, :] for k in range(n)]
        xi = [xs[k, im, :] for k in range(n)]
        gr = [gs[k, re, :] for k in range(n)]
        gi = [gs[k, im, :] for k in range(n)]
        xt = [a + b for a, b in zip(xr, xi)]
        gt = [a + b for a, b in zip(gr, gi)]
        for i in range(n):
            one = xr[0] * gr[i]
            two = xi[0] * gi[i]
            three = xt[0] * gt[i]
            for k in range(1, i + 1):
                one += xr[k] * gr[i - k]
                two += xi[k] * gi[i - k]
                three += xt[k] * gt[i - k]
            ys[i, re, :] = one - two
            ys[i, im, :] = three - (one + two)

    for i in range(n):
        conv = jnp.dot(inv_ref[...], ys[i].astype(jnp.bfloat16), preferred_element_type=f32)
        mix = outer_ref[i].astype(f32) * (conv + skip_ref[...] * gf_ref[i, 0].astype(f32))
        mix_ref[i * block : (i + 1) * block, :] = mix.astype(jnp.bfloat16)


def convolve(pair, outer, skip):
    n, _, block, chans = pair.shape
    forward, inverse = tables(block)
    return pl.pallas_call(
        conv_kernel,
        out_shape=jax.ShapeDtypeStruct((n * block, chans), jnp.bfloat16),
        scratch_shapes=[pltpu.VMEM((n, 2 * block, chans), jnp.float32)] * 3,
        compiler_params=pltpu.CompilerParams(vmem_limit_bytes=40 * 2**20),
        name="convolve",
    )(pair, outer, skip, jnp.asarray(forward), jnp.asarray(inverse))


def per_device(outer_gate, inner_gate, values_in, filters, skip_gain, w_out):
    n, m = lax.axis_size("ctx"), lax.axis_size("ch")
    j, k = lax.axis_index("ctx"), lax.axis_index("ch")
    block, wide = outer_gate.shape
    chans = wide // n
    gated = (inner_gate.astype(jnp.float32) * values_in.astype(jnp.float32)).astype(jnp.bfloat16)

    def cut(rows):
        return rows.reshape(block, n, chans).transpose(1, 0, 2)

    pair = jnp.stack([cut(gated), cut(filters.astype(jnp.bfloat16))], axis=1)
    pair = lax.all_to_all(pair, "ctx", 0, 0)
    outer = lax.all_to_all(cut(outer_gate), "ctx", 0, 0)
    skip = lax.dynamic_slice_in_dim(skip_gain, j * chans, chans, 0)[None, :]
    mix = convolve(pair, outer, skip)
    whole = lax.all_gather(mix, "ctx", axis=1, tiled=True)
    part = jnp.dot(whole, w_out, preferred_element_type=jnp.float32).astype(jnp.bfloat16)
    bit = 1
    groups = part.reshape((m, -1, part.shape[1]))
    while bit < m:
        mine = (k // bit) % 2
        split = groups.reshape((groups.shape[0] // 2, 2) + groups.shape[1:])
        keep = lax.dynamic_index_in_dim(split, mine, 1, keepdims=False)
        give = lax.dynamic_index_in_dim(split, 1 - mine, 1, keepdims=False)
        got = lax.ppermute(give, "ch", [(d, d ^ bit) for d in range(m)])
        groups = (keep.astype(jnp.float32) + got.astype(jnp.float32)).astype(jnp.bfloat16)
        bit *= 2
    q = n // m
    rows = groups.reshape(q, block, part.shape[1])
    found = []
    for e in range(q):
        sent = lax.dynamic_index_in_dim(rows, (j + e) % q, 0, keepdims=False)
        route = []
        for a in range(n):
            for b in range(m):
                route.append((a * m + b, (q * b + (a + e) % q) * m + a // q))
        found.append(lax.ppermute(sent, ("ctx", "ch"), route))
    columns = [
        lax.select_n((j - h) % q, *found) if q > 1 else found[0] for h in range(q)
    ]
    return jnp.concatenate(columns, axis=1)


def solution(mesh):
    placed = (
        P("ctx", "ch"),
        P("ctx", "ch"),
        P("ctx", "ch"),
        P("ctx", "ch"),
        P("ch"),
        P("ch", "ctx"),
    )
    return jax.shard_map(
        per_device, mesh=mesh, in_specs=placed, out_specs=P("ctx", "ch"), check_vma=False
    )
```

```python
import math

import jax
import jax.numpy as jnp
import numpy as np
from jax import lax
from jax.experimental import pallas as pl
from jax.experimental.pallas import tpu as pltpu
from jax.sharding import PartitionSpec as P

BF16, F32 = jnp.bfloat16, jnp.float32
MIB = 2**20


def tables(block):
    freqs = np.arange(block, dtype=np.float64)[:, None] + 0.5
    window = np.arange(-block, block, dtype=np.float64)[None, :]
    angles = math.pi / block * freqs * window
    forward = np.concatenate([np.cos(angles), -np.sin(angles)], axis=0)
    places = angles[:, block:].T
    inverse = np.concatenate([np.cos(places), -np.sin(places)], axis=1) / block
    return forward.astype(BF16), inverse.astype(BF16)


def pack_kernel(outer_ref, inner_ref, values_ref, filters_ref, out_ref):
    n, _, _, chans = out_ref.shape
    gated = (inner_ref[...].astype(F32) * values_ref[...].astype(F32)).astype(BF16)
    lags = filters_ref[...].astype(BF16)
    outer = outer_ref[...]
    for d in range(n):
        part = slice(d * chans, (d + 1) * chans)
        out_ref[d, 0] = gated[:, part]
        out_ref[d, 1] = lags[:, part]
        out_ref[d, 2] = outer[:, part]


def pack(outer_gate, inner_gate, values_in, filters, n):
    block, wide = outer_gate.shape
    tile = block // 2
    return pl.pallas_call(
        pack_kernel,
        grid=(block // tile,),
        in_specs=[pl.BlockSpec((tile, wide), lambda t: (t, 0))] * 4,
        out_specs=pl.BlockSpec((n, 3, tile, wide // n), lambda t: (0, 0, t, 0)),
        out_shape=jax.ShapeDtypeStruct((n, 3, block, wide // n), BF16),
        compiler_params=pltpu.CompilerParams(vmem_limit_bytes=32 * MIB),
        cost_estimate=pl.CostEstimate(flops=2**18, bytes_accessed=4 * MIB, transcendentals=0),
        name="pack",
    )(outer_gate, inner_gate, values_in, filters)


def conv_kernel(places, in_ref, skip_ref, fwd_ref, inv_ref, *rest):
    mixes, (xs, gs, ys) = rest[:-3], rest[-3:]
    n, _, block, chans = in_ref.shape
    for k in range(n):
        xs[k] = jnp.dot(fwd_ref[:, block:], in_ref[k, 0], preferred_element_type=F32)
        lag = jnp.dot(fwd_ref[:, block:], in_ref[k, 1], preferred_element_type=F32)
        if k:
            lag += jnp.dot(fwd_ref[:, :block], in_ref[k - 1, 1], preferred_element_type=F32)
        gs[k] = lag

    step = 8

    @pl.loop(0, block // step)
    def _(c):
        re = pl.ds(pl.multiple_of(c * step, step), step)
        im = pl.ds(pl.multiple_of(block + c * step, step), step)
        xr = [xs[k, re, :] for k in range(n)]
        xi = [xs[k, im, :] for k in range(n)]
        gr = [gs[k, re, :] for k in range(n)]
        gi = [gs[k, im, :] for k in range(n)]
        xt = [a + b for a, b in zip(xr, xi)]
        gt = [a + b for a, b in zip(gr, gi)]
        for i in range(n):
            one = xr[0] * gr[i]
            two = xi[0] * gi[i]
            three = xt[0] * gt[i]
            for k in range(1, i + 1):
                one += xr[k] * gr[i - k]
                two += xi[k] * gi[i - k]
                three += xt[k] * gt[i - k]
            ys[i, re, :] = one - two
            ys[i, im, :] = three - (one + two)

    for i in range(n):
        conv = jnp.dot(inv_ref[...], ys[i].astype(BF16), preferred_element_type=F32)
        mix = in_ref[i, 2].astype(F32) * (conv + skip_ref[...] * in_ref[i, 0].astype(F32))
        chunk, place = places[i]
        mixes[chunk][place * block : (place + 1) * block, :] = mix.astype(BF16)


def convolve(packed, skip, places):
    n, _, block, chans = packed.shape
    forward, inverse = tables(block)
    return pl.pallas_call(
        lambda *refs: conv_kernel(places, *refs),
        out_shape=[jax.ShapeDtypeStruct((n // 2 * block, chans), BF16)] * 2,
        scratch_shapes=[pltpu.VMEM((n, 2 * block, chans), F32)] * 3,
        compiler_params=pltpu.CompilerParams(vmem_limit_bytes=40 * MIB),
        cost_estimate=pl.CostEstimate(flops=2**31, bytes_accessed=4 * MIB, transcendentals=0),
        name="convolve",
    )(packed, skip, jnp.asarray(forward), jnp.asarray(inverse))


def project_kernel(rows_ref, owners_ref, *refs):
    pieces, (w_ref, keep_ref, give_ref) = refs[:-3], refs[-3:]
    total = None
    for s in range(0, len(pieces), 2):
        left = jnp.concatenate([piece[...] for piece in pieces[s : s + 2]], axis=1)
        right = jnp.concatenate([w_ref[owners_ref[t]] for t in range(s, s + 2)], axis=0)
        term = jnp.dot(left, right, preferred_element_type=F32)
        total = term if total is None else total + term
    t = pl.program_id(0)
    half = pl.num_programs(0) // 2

    @pl.when(t < half)
    def _():
        give_ref[...] = total.astype(BF16)

    @pl.when(t >= half)
    def _():
        keep_ref[...] = total.astype(BF16)


def project(pieces, owners, w_out, order, block):
    n = len(pieces)
    chans = pieces[0].shape[1]
    count = order.shape[0]
    half = count // 2
    columns = w_out.shape[1]
    part = jax.ShapeDtypeStruct((half * block, columns), BF16)
    return pl.pallas_call(
        project_kernel,
        grid_spec=pltpu.PrefetchScalarGridSpec(
            num_scalar_prefetch=2,
            grid=(count,),
            in_specs=[pl.BlockSpec((block, chans), lambda t, o, w: (o[t], 0))] * n
            + [pl.BlockSpec((n, chans, columns), lambda t, o, w: (0, 0, 0))],
            out_specs=[
                pl.BlockSpec((block, columns), lambda t, o, w: (jnp.maximum(t - half, 0), 0)),
                pl.BlockSpec((block, columns), lambda t, o, w: (jnp.minimum(t, half - 1), 0)),
            ],
        ),
        out_shape=[part, part],
        compiler_params=pltpu.CompilerParams(vmem_limit_bytes=32 * MIB),
        cost_estimate=pl.CostEstimate(
            flops=2 * count * block * n * chans * columns,
            bytes_accessed=4 * MIB,
            transcendentals=0,
        ),
        name="project",
    )(order, owners, *pieces, w_out.reshape(n, chans, columns))


def ring_of(deep, across):
    walk = []
    for a in range(across):
        column = list(range(1, deep))
        walk += [d * across + a for d in (column if a % 2 == 0 else column[::-1])]
    return walk + [a for a in reversed(range(across))]


def per_device(outer_gate, inner_gate, values_in, filters, skip_gain, w_out):
    n, m = lax.axis_size("ctx"), lax.axis_size("ch")
    j, k = lax.axis_index("ctx"), lax.axis_index("ch")
    block, wide = outer_gate.shape
    chans = wide // n
    across = n // 4
    q = n // m

    of = [[(h + 2 * deep) * across + a for deep in range(2) for a in range(across)] for h in range(2)]
    places = {r: (h, b) for h in range(2) for b, r in enumerate(of[h])}

    packed = pack(outer_gate, inner_gate, values_in, filters, n)
    packed = lax.all_to_all(packed, "ctx", 0, 0)
    skip = lax.dynamic_slice_in_dim(skip_gain, j * chans, chans, 0)[None, :]
    mixes = convolve(packed, skip, places)

    ring = ring_of(4, across)
    spot = np.argsort(np.array(ring))
    onward = [(ring[p], ring[(p + 1) % n]) for p in range(n)]
    back = [(b, a) for a, b in onward]
    me = jnp.asarray(spot.astype(np.int32))[j]
    ring_table = jnp.asarray(np.array(ring, np.int32))

    hops = [(n // 2, n // 2 - 1), (n // 2 - 1, n // 2)]
    pieces = [[mix] for mix in mixes]
    offsets = [[0], [0]]
    tips = [[mix, mix] for mix in mixes]
    for s in range(n // 2):
        for h in range(2):
            for way, route in enumerate((onward, back)):
                if s < hops[h][way]:
                    tips[h][way] = lax.ppermute(tips[h][way], "ctx", route)
                    pieces[h].append(tips[h][way])
                    offsets[h].append(-(s + 1) if way == 0 else s + 1)

    half = m // 2
    core = k % 2
    swap = [(d, d ^ 1) for d in range(m)]
    order = (jnp.arange(m, dtype=jnp.int32) + (1 - core) * half) % m
    ended = []
    for h in range(2):
        owners = ring_table[(me + jnp.array(offsets[h], jnp.int32)) % n]
        keep, give = project(pieces[h], owners, w_out, order, block)
        got = lax.ppermute(give, "ch", swap)
        kept = (keep.astype(F32) + got.astype(F32)).reshape(half, block, -1)
        bit = 1
        while bit < half:
            mine = (k // 2 // bit) % 2
            split = kept.reshape((kept.shape[0] // 2, 2) + kept.shape[1:])
            keep = lax.dynamic_index_in_dim(split, mine, 1, keepdims=False)
            give = lax.dynamic_index_in_dim(split, 1 - mine, 1, keepdims=False).astype(BF16)
            got = lax.ppermute(give, "ch", [(d, d ^ (2 * bit)) for d in range(m)])
            kept = keep + got.astype(F32)
            bit *= 2
        ended.append(kept[0].astype(BF16))

    columns = []
    for c in range(q):
        found = []
        for h in range(2):
            route = []
            for a in range(c, n, q):
                for b in range(m):
                    r = of[h][(b % 2) * half + b // 2]
                    route.append((a * m + b, r * m + a // q))
            found.append(lax.ppermute(ended[h], ("ctx", "ch"), route))
        columns.append(jnp.where((j // across) % 2 == 0, found[0], found[1]))
    return jnp.concatenate(columns, axis=1)


def solution(mesh):
    placed = (
        P("ctx", "ch"),
        P("ctx", "ch"),
        P("ctx", "ch"),
        P("ctx", "ch"),
        P("ch"),
        P("ch", "ctx"),
    )
    return jax.shard_map(
        per_device, mesh=mesh, in_specs=placed, out_specs=P("ctx", "ch"), check_vma=False
    )
```

```python
import math

import jax
import jax.numpy as jnp
import numpy as np
from jax import lax
from jax.experimental import pallas as pl
from jax.experimental.pallas import tpu as pltpu
from jax.sharding import PartitionSpec as P

BF16, F32 = jnp.bfloat16, jnp.float32
MIB = 2**20


def tables(block):
    freqs = np.arange(block, dtype=np.float64)[:, None] + 0.5
    window = np.arange(-block, block, dtype=np.float64)[None, :]
    angles = math.pi / block * freqs * window
    forward = np.concatenate([np.cos(angles), -np.sin(angles)], axis=0)
    places = angles[:, block:].T
    inverse = np.concatenate([np.cos(places), -np.sin(places)], axis=1) / block
    return forward.astype(BF16), inverse.astype(BF16)


def pack_kernel(outer_ref, inner_ref, values_ref, filters_ref, out_ref):
    n, _, _, chans = out_ref.shape
    gated = (inner_ref[...].astype(F32) * values_ref[...].astype(F32)).astype(BF16)
    lags = filters_ref[...].astype(BF16)
    outer = outer_ref[...]
    for d in range(n):
        part = slice(d * chans, (d + 1) * chans)
        out_ref[d, 0] = gated[:, part]
        out_ref[d, 1] = lags[:, part]
        out_ref[d, 2] = outer[:, part]


def pack(outer_gate, inner_gate, values_in, filters, n):
    block, wide = outer_gate.shape
    tile = block // 2
    return pl.pallas_call(
        pack_kernel,
        grid=(block // tile,),
        in_specs=[pl.BlockSpec((tile, wide), lambda t: (t, 0))] * 4,
        out_specs=pl.BlockSpec((n, 3, tile, wide // n), lambda t: (0, 0, t, 0)),
        out_shape=jax.ShapeDtypeStruct((n, 3, block, wide // n), BF16),
        compiler_params=pltpu.CompilerParams(vmem_limit_bytes=60 * MIB),
        cost_estimate=pl.CostEstimate(flops=2**18, bytes_accessed=4 * MIB, transcendentals=0),
        name="pack",
    )(outer_gate, inner_gate, values_in, filters)


def conv_kernel(places, in_ref, skip_ref, fwd_ref, inv_ref, *rest):
    mixes, (xs, gs, ys) = rest[:-3], rest[-3:]
    n, _, block, chans = in_ref.shape
    for k in range(n):
        xs[k] = jnp.dot(fwd_ref[:, block:], in_ref[k, 0], preferred_element_type=F32)
        lag = jnp.dot(fwd_ref[:, block:], in_ref[k, 1], preferred_element_type=F32)
        if k:
            lag += jnp.dot(fwd_ref[:, :block], in_ref[k - 1, 1], preferred_element_type=F32)
        gs[k] = lag

    step = 8

    @pl.loop(0, block // step)
    def _(c):
        re = pl.ds(pl.multiple_of(c * step, step), step)
        im = pl.ds(pl.multiple_of(block + c * step, step), step)
        xr = [xs[k, re, :] for k in range(n)]
        xi = [xs[k, im, :] for k in range(n)]
        gr = [gs[k, re, :] for k in range(n)]
        gi = [gs[k, im, :] for k in range(n)]
        xt = [a + b for a, b in zip(xr, xi)]
        gt = [a + b for a, b in zip(gr, gi)]
        for i in range(n):
            one = xr[0] * gr[i]
            two = xi[0] * gi[i]
            three = xt[0] * gt[i]
            for k in range(1, i + 1):
                one += xr[k] * gr[i - k]
                two += xi[k] * gi[i - k]
                three += xt[k] * gt[i - k]
            ys[i, re, :] = one - two
            ys[i, im, :] = three - (one + two)

    for i in range(n):
        conv = jnp.dot(inv_ref[...], ys[i].astype(BF16), preferred_element_type=F32)
        mix = in_ref[i, 2].astype(F32) * (conv + skip_ref[...] * in_ref[i, 0].astype(F32))
        chunk, place = places[i]
        mixes[chunk][place * block : (place + 1) * block, :] = mix.astype(BF16)


def convolve(packed, skip, places):
    n, _, block, chans = packed.shape
    forward, inverse = tables(block)
    return pl.pallas_call(
        lambda *refs: conv_kernel(places, *refs),
        out_shape=[jax.ShapeDtypeStruct((n // 2 * block, chans), BF16)] * 2,
        scratch_shapes=[pltpu.VMEM((n, 2 * block, chans), F32)] * 3,
        compiler_params=pltpu.CompilerParams(vmem_limit_bytes=16 * MIB),
        cost_estimate=pl.CostEstimate(flops=2**31, bytes_accessed=4 * MIB, transcendentals=0),
        name="convolve",
    )(packed, skip, jnp.asarray(forward), jnp.asarray(inverse))


def project_kernel(here_ref, table_ref, *refs):
    pieces, (w_ref, keep_ref, give_ref) = refs[:-3], refs[-3:]
    n = len(pieces)
    total = None
    for s in range(0, len(pieces), 2):
        left = jnp.concatenate([piece[...] for piece in pieces[s : s + 2]], axis=1)
        right = jnp.concatenate([w_ref[table_ref[here_ref[0] * n + t]] for t in range(s, s + 2)], axis=0)
        term = jnp.dot(left, right, preferred_element_type=F32)
        total = term if total is None else total + term
    t = pl.program_id(0)
    half = pl.num_programs(0) // 2

    @pl.when(t < half)
    def _():
        give_ref[...] = total.astype(BF16)

    @pl.when(t >= half)
    def _():
        keep_ref[...] = total.astype(BF16)


def project(pieces, here, table, w_out, block):
    n = len(pieces)
    count = pieces[0].shape[0] // block
    chans = pieces[0].shape[1]
    half = count // 2

    def rows(t, here, table):
        return (lax.rem(t + (1 - lax.rem(here[1], 2)) * half, count), 0)

    columns = w_out.shape[1]
    part = jax.ShapeDtypeStruct((half * block, columns), BF16)
    return pl.pallas_call(
        project_kernel,
        grid_spec=pltpu.PrefetchScalarGridSpec(
            num_scalar_prefetch=2,
            grid=(count,),
            in_specs=[pl.BlockSpec((block, chans), rows)] * n
            + [pl.BlockSpec((n, chans, columns), lambda t, o, w: (0, 0, 0))],
            out_specs=[
                pl.BlockSpec((block, columns), lambda t, o, w: (jnp.maximum(t - half, 0), 0)),
                pl.BlockSpec((block, columns), lambda t, o, w: (jnp.minimum(t, half - 1), 0)),
            ],
        ),
        out_shape=[part, part],
        compiler_params=pltpu.CompilerParams(vmem_limit_bytes=10 * MIB),
        cost_estimate=pl.CostEstimate(
            flops=2 * count * block * n * chans * columns,
            bytes_accessed=4 * MIB,
            transcendentals=0,
        ),
        name="project",
    )(here, table, *pieces, w_out.reshape(n, chans, columns))


def ring_of(deep, across):
    walk = []
    for a in range(across):
        column = list(range(1, deep))
        walk += [d * across + a for d in (column if a % 2 == 0 else column[::-1])]
    return walk + [a for a in reversed(range(across))]


def per_device(outer_gate, inner_gate, values_in, filters, skip_gain, w_out):
    n, m = lax.axis_size("ctx"), lax.axis_size("ch")
    j, k = lax.axis_index("ctx"), lax.axis_index("ch")
    block, wide = outer_gate.shape
    chans = wide // n
    across = n // 4
    q = n // m

    of = [[(h + 2 * deep) * across + a for deep in range(2) for a in range(across)] for h in range(2)]
    places = {r: (h, b) for h in range(2) for b, r in enumerate(of[h])}

    packed = pack(outer_gate, inner_gate, values_in, filters, n)
    packed = lax.all_to_all(packed, "ctx", 0, 0)
    skip = lax.dynamic_slice_in_dim(skip_gain, j * chans, chans, 0)[None, :]
    mixes = convolve(packed, skip, places)

    ring = ring_of(4, across)
    spot = np.argsort(np.array(ring))
    onward = [(ring[p], ring[(p + 1) % n]) for p in range(n)]
    back = [(b, a) for a, b in onward]
    here = jnp.stack([j, k]).astype(jnp.int32)

    hops = [(n // 2, n // 2 - 1), (n // 2 - 1, n // 2)]
    pieces = [[mix] for mix in mixes]
    offsets = [[0], [0]]
    tips = [[mix, mix] for mix in mixes]
    for s in range(n // 2):
        for h in range(2):
            for way, route in enumerate((onward, back)):
                if s < hops[h][way]:
                    tips[h][way] = lax.ppermute(tips[h][way], "ctx", route)
                    pieces[h].append(tips[h][way])
                    offsets[h].append(-(s + 1) if way == 0 else s + 1)

    half = m // 2
    swap = [(d, d ^ 1) for d in range(m)]
    ended = []
    for h in range(2):
        owners = np.array([[ring[(spot[a] + o) % n] for o in offsets[h]] for a in range(n)], np.int32)
        keep, give = project(pieces[h], here, jnp.asarray(owners.reshape(-1)), w_out, block)
        got = lax.ppermute(give, "ch", swap)
        kept = (keep.astype(F32) + got.astype(F32)).reshape(half, block, -1)
        bit = 1
        while bit < half:
            mine = (k // 2 // bit) % 2
            split = kept.reshape((kept.shape[0] // 2, 2) + kept.shape[1:])
            keep = lax.dynamic_index_in_dim(split, mine, 1, keepdims=False)
            give = lax.dynamic_index_in_dim(split, 1 - mine, 1, keepdims=False).astype(BF16)
            got = lax.ppermute(give, "ch", [(d, d ^ (2 * bit)) for d in range(m)])
            kept = keep + got.astype(F32)
            bit *= 2
        ended.append(kept[0].astype(BF16))

    columns = []
    for c in range(q):
        found = []
        for h in range(2):
            route = []
            for a in range(c, n, q):
                for b in range(m):
                    r = of[h][(b % 2) * half + b // 2]
                    route.append((a * m + b, r * m + a // q))
            found.append(lax.ppermute(ended[h], ("ctx", "ch"), route))
        columns.append(jnp.where((j // across) % 2 == 0, found[0], found[1]))
    return jnp.concatenate(columns, axis=1)


def solution(mesh):
    placed = (
        P("ctx", "ch"),
        P("ctx", "ch"),
        P("ctx", "ch"),
        P("ctx", "ch"),
        P("ch"),
        P("ch", "ctx"),
    )
    return jax.shard_map(
        per_device, mesh=mesh, in_specs=placed, out_specs=P("ctx", "ch"), check_vma=False
    )
```

```python
import math

import jax
import jax.numpy as jnp
import numpy as np
from jax import lax
from jax.experimental import pallas as pl
from jax.experimental.pallas import tpu as pltpu
from jax.sharding import PartitionSpec as P

BF16, F32 = jnp.bfloat16, jnp.float32
MIB = 2**20


def tables(block):
    freqs = np.arange(block, dtype=np.float64)[:, None] + 0.5
    window = np.arange(-block, block, dtype=np.float64)[None, :]
    angles = math.pi / block * freqs * window
    forward = np.concatenate([np.cos(angles), -np.sin(angles)], axis=0)
    places = angles[:, block:].T
    inverse = np.concatenate([np.cos(places), -np.sin(places)], axis=1) / block
    return forward.astype(BF16), inverse.astype(BF16)


def pack_kernel(outer_ref, inner_ref, values_ref, filters_ref, out_ref):
    n, _, _, chans = out_ref.shape
    gated = (inner_ref[...].astype(F32) * values_ref[...].astype(F32)).astype(BF16)
    lags = filters_ref[...].astype(BF16)
    outer = outer_ref[...]
    for d in range(n):
        part = slice(d * chans, (d + 1) * chans)
        out_ref[d, 0] = gated[:, part]
        out_ref[d, 1] = lags[:, part]
        out_ref[d, 2] = outer[:, part]


def pack(outer_gate, inner_gate, values_in, filters, n):
    block, wide = outer_gate.shape
    tile = block // 2
    return pl.pallas_call(
        pack_kernel,
        grid=(block // tile,),
        in_specs=[pl.BlockSpec((tile, wide), lambda t: (t, 0))] * 4,
        out_specs=pl.BlockSpec((n, 3, tile, wide // n), lambda t: (0, 0, t, 0)),
        out_shape=jax.ShapeDtypeStruct((n, 3, block, wide // n), BF16),
        compiler_params=pltpu.CompilerParams(vmem_limit_bytes=60 * MIB),
        cost_estimate=pl.CostEstimate(flops=2**18, bytes_accessed=4 * MIB, transcendentals=0),
        name="pack",
    )(outer_gate, inner_gate, values_in, filters)


def conv_kernel(places, in_ref, skip_ref, fwd_ref, inv_ref, *rest):
    mixes, (xs, gs, ys) = rest[:-3], rest[-3:]
    n, _, block, chans = in_ref.shape
    for k in range(n):
        xs[k] = jnp.dot(fwd_ref[:, block:], in_ref[k, 0], preferred_element_type=F32)
        lag = jnp.dot(fwd_ref[:, block:], in_ref[k, 1], preferred_element_type=F32)
        if k:
            lag += jnp.dot(fwd_ref[:, :block], in_ref[k - 1, 1], preferred_element_type=F32)
        gs[k] = lag

    step = 8

    @pl.loop(0, block // step)
    def _(c):
        re = pl.ds(pl.multiple_of(c * step, step), step)
        im = pl.ds(pl.multiple_of(block + c * step, step), step)
        xr = [xs[k, re, :] for k in range(n)]
        xi = [xs[k, im, :] for k in range(n)]
        gr = [gs[k, re, :] for k in range(n)]
        gi = [gs[k, im, :] for k in range(n)]
        xt = [a + b for a, b in zip(xr, xi)]
        gt = [a + b for a, b in zip(gr, gi)]
        for i in range(n):
            one = xr[0] * gr[i]
            two = xi[0] * gi[i]
            three = xt[0] * gt[i]
            for k in range(1, i + 1):
                one += xr[k] * gr[i - k]
                two += xi[k] * gi[i - k]
                three += xt[k] * gt[i - k]
            ys[i, re, :] = one - two
            ys[i, im, :] = three - (one + two)

    for i in range(n):
        conv = jnp.dot(inv_ref[...], ys[i].astype(BF16), preferred_element_type=F32)
        mix = in_ref[i, 2].astype(F32) * (conv + skip_ref[...] * in_ref[i, 0].astype(F32))
        chunk, place = places[i]
        mixes[chunk][place * block : (place + 1) * block, :] = mix.astype(BF16)


def convolve(packed, skip, places):
    n, _, block, chans = packed.shape
    forward, inverse = tables(block)
    return pl.pallas_call(
        lambda *refs: conv_kernel(places, *refs),
        out_shape=[jax.ShapeDtypeStruct((n // 2 * block, chans), BF16)] * 2,
        scratch_shapes=[pltpu.VMEM((n, 2 * block, chans), F32)] * 3,
        compiler_params=pltpu.CompilerParams(vmem_limit_bytes=16 * MIB),
        cost_estimate=pl.CostEstimate(flops=2**31, bytes_accessed=4 * MIB, transcendentals=0),
        name="convolve",
    )(packed, skip, jnp.asarray(forward), jnp.asarray(inverse))


def project_kernel(here_ref, table_ref, *refs):
    pieces, (w_ref, keep_ref, give_ref) = refs[:-3], refs[-3:]
    n = len(pieces)
    total = None
    for s in range(0, len(pieces), 2):
        left = jnp.concatenate([piece[...] for piece in pieces[s : s + 2]], axis=1)
        right = jnp.concatenate([w_ref[table_ref[here_ref[0] * n + t]] for t in range(s, s + 2)], axis=0)
        term = jnp.dot(left, right, preferred_element_type=F32)
        total = term if total is None else total + term
    t = pl.program_id(0)
    half = pl.num_programs(0) // 2

    @pl.when(t < half)
    def _():
        give_ref[...] = total.astype(BF16)

    @pl.when(t >= half)
    def _():
        keep_ref[...] = total.astype(BF16)


def project(pieces, here, table, w_out, block):
    n = len(pieces)
    count = pieces[0].shape[0] // block
    chans = pieces[0].shape[1]
    half = count // 2

    def rows(t, here, table):
        return (lax.rem(t + (1 - lax.rem(here[1], 2)) * half, count), 0)

    columns = w_out.shape[1]
    part = jax.ShapeDtypeStruct((half * block, columns), BF16)
    return pl.pallas_call(
        project_kernel,
        grid_spec=pltpu.PrefetchScalarGridSpec(
            num_scalar_prefetch=2,
            grid=(count,),
            in_specs=[pl.BlockSpec((block, chans), rows)] * n
            + [pl.BlockSpec((n, chans, columns), lambda t, o, w: (0, 0, 0))],
            out_specs=[
                pl.BlockSpec((block, columns), lambda t, o, w: (jnp.maximum(t - half, 0), 0)),
                pl.BlockSpec((block, columns), lambda t, o, w: (jnp.minimum(t, half - 1), 0)),
            ],
        ),
        out_shape=[part, part],
        compiler_params=pltpu.CompilerParams(vmem_limit_bytes=60 * MIB),
        cost_estimate=pl.CostEstimate(flops=0, bytes_accessed=0, transcendentals=0),
        name="project",
    )(here, table, *pieces, w_out.reshape(n, chans, columns))


def ring_of(deep, across):
    walk = []
    for a in range(across):
        column = list(range(1, deep))
        walk += [d * across + a for d in (column if a % 2 == 0 else column[::-1])]
    return walk + [a for a in reversed(range(across))]


def per_device(outer_gate, inner_gate, values_in, filters, skip_gain, w_out):
    n, m = lax.axis_size("ctx"), lax.axis_size("ch")
    j, k = lax.axis_index("ctx"), lax.axis_index("ch")
    block, wide = outer_gate.shape
    chans = wide // n
    across = n // 4
    q = n // m

    of = [[(h + 2 * deep) * across + a for deep in range(2) for a in range(across)] for h in range(2)]
    places = {r: (h, b) for h in range(2) for b, r in enumerate(of[h])}

    packed = pack(outer_gate, inner_gate, values_in, filters, n)
    packed = lax.all_to_all(packed, "ctx", 0, 0)
    skip = lax.dynamic_slice_in_dim(skip_gain, j * chans, chans, 0)[None, :]
    mixes = convolve(packed, skip, places)

    ring = ring_of(4, across)
    spot = np.argsort(np.array(ring))
    onward = [(ring[p], ring[(p + 1) % n]) for p in range(n)]
    back = [(b, a) for a, b in onward]
    here = jnp.stack([j, k]).astype(jnp.int32)

    hops = [(n // 2, n // 2 - 1), (n // 2 - 1, n // 2)]
    pieces = [[mix] for mix in mixes]
    offsets = [[0], [0]]
    tips = [[mix, mix] for mix in mixes]
    late = []
    for s in range(n // 2):
        if s >= 2:
            tied = lax.optimization_barrier((*tips[0], *late[s - 1]))
            tips[0] = list(tied[:2])
        late.append(list(tips[1]))
        for h in range(2):
            for way, route in enumerate((onward, back)):
                if s < hops[h][way]:
                    tips[h][way] = lax.ppermute(tips[h][way], "ctx", route)
                    pieces[h].append(tips[h][way])
                    offsets[h].append(-(s + 1) if way == 0 else s + 1)

    half = m // 2
    swap = [(d, d ^ 1) for d in range(m)]
    placed = [[], []]
    gate = []
    for h in range(2):
        ahead = late[-1] if h == 0 else gate
        pieces[h][-1], *_ = lax.optimization_barrier((pieces[h][-1], *ahead))
        owners = np.array([[ring[(spot[a] + o) % n] for o in offsets[h]] for a in range(n)], np.int32)
        keep, give = project(pieces[h], here, jnp.asarray(owners.reshape(-1)), w_out, block)
        got = lax.ppermute(give, "ch", swap)
        got, *_ = lax.optimization_barrier((got, pieces[1][-1] if h == 0 else ended))
        kept = (keep.astype(F32) + got.astype(F32)).reshape(half, block, -1)
        bit = 1
        while bit < half:
            mine = (k // 2 // bit) % 2
            split = kept.reshape((kept.shape[0] // 2, 2) + kept.shape[1:])
            keep = lax.dynamic_index_in_dim(split, mine, 1, keepdims=False)
            give = lax.dynamic_index_in_dim(split, 1 - mine, 1, keepdims=False).astype(BF16)
            gate = [give]
            got = lax.ppermute(give, "ch", [(d, d ^ (2 * bit)) for d in range(m)])
            if h:
                got, *_ = lax.optimization_barrier((got, *placed[0]))
            kept = keep + got.astype(F32)
            bit *= 2
        ended = kept[0].astype(BF16)
        for c in range(q):
            route = []
            for a in range(c, n, q):
                for b in range(m):
                    r = of[h][(b % 2) * half + b // 2]
                    route.append((a * m + b, r * m + a // q))
            placed[h].append(lax.ppermute(ended, ("ctx", "ch"), route))

    even = (j // across) % 2 == 0
    return jnp.concatenate([jnp.where(even, a, b) for a, b in zip(*placed)], axis=1)


def solution(mesh):
    placed = (
        P("ctx", "ch"),
        P("ctx", "ch"),
        P("ctx", "ch"),
        P("ctx", "ch"),
        P("ch"),
        P("ch", "ctx"),
    )
    return jax.shard_map(
        per_device, mesh=mesh, in_specs=placed, out_specs=P("ctx", "ch"), check_vma=False
    )
```

```python
import math

import jax
import jax.numpy as jnp
import numpy as np
from jax import lax
from jax.experimental import pallas as pl
from jax.experimental.pallas import tpu as pltpu
from jax.sharding import PartitionSpec as P

BF16, F32 = jnp.bfloat16, jnp.float32
MIB = 2**20


def tables(block):
    freqs = np.arange(block, dtype=np.float64)[:, None] + 0.5
    window = np.arange(-block, block, dtype=np.float64)[None, :]
    angles = math.pi / block * freqs * window
    forward = np.concatenate([np.cos(angles), -np.sin(angles)], axis=0)
    places = angles[:, block:].T
    inverse = np.concatenate([np.cos(places), -np.sin(places)], axis=1) / block
    return forward.astype(BF16), inverse.astype(BF16)


def pack_kernel(outer_ref, inner_ref, values_ref, filters_ref, out_ref):
    n, _, _, chans = out_ref.shape
    gated = (inner_ref[...].astype(F32) * values_ref[...].astype(F32)).astype(BF16)
    lags = filters_ref[...].astype(BF16)
    outer = outer_ref[...]
    for d in range(n):
        part = slice(d * chans, (d + 1) * chans)
        out_ref[d, 0] = gated[:, part]
        out_ref[d, 1] = lags[:, part]
        out_ref[d, 2] = outer[:, part]


def pack(outer_gate, inner_gate, values_in, filters, n):
    block, wide = outer_gate.shape
    tile = block // 2
    return pl.pallas_call(
        pack_kernel,
        grid=(block // tile,),
        in_specs=[pl.BlockSpec((tile, wide), lambda t: (t, 0))] * 4,
        out_specs=pl.BlockSpec((n, 3, tile, wide // n), lambda t: (0, 0, t, 0)),
        out_shape=jax.ShapeDtypeStruct((n, 3, block, wide // n), BF16),
        compiler_params=pltpu.CompilerParams(vmem_limit_bytes=60 * MIB),
        cost_estimate=pl.CostEstimate(flops=2**18, bytes_accessed=4 * MIB, transcendentals=0),
        name="pack",
    )(outer_gate, inner_gate, values_in, filters)


def conv_kernel(places, in_ref, skip_ref, fwd_ref, inv_ref, *rest):
    mixes, (xs, gs, ys) = rest[:-3], rest[-3:]
    n, _, block, chans = in_ref.shape
    for k in range(n):
        xs[k] = jnp.dot(fwd_ref[:, block:], in_ref[k, 0], preferred_element_type=F32)
        lag = jnp.dot(fwd_ref[:, block:], in_ref[k, 1], preferred_element_type=F32)
        if k:
            lag += jnp.dot(fwd_ref[:, :block], in_ref[k - 1, 1], preferred_element_type=F32)
        gs[k] = lag

    step = 8

    @pl.loop(0, block // step)
    def _(c):
        re = pl.ds(pl.multiple_of(c * step, step), step)
        im = pl.ds(pl.multiple_of(block + c * step, step), step)
        xr = [xs[k, re, :] for k in range(n)]
        xi = [xs[k, im, :] for k in range(n)]
        gr = [gs[k, re, :] for k in range(n)]
        gi = [gs[k, im, :] for k in range(n)]
        xt = [a + b for a, b in zip(xr, xi)]
        gt = [a + b for a, b in zip(gr, gi)]
        for i in range(n):
            one = xr[0] * gr[i]
            two = xi[0] * gi[i]
            three = xt[0] * gt[i]
            for k in range(1, i + 1):
                one += xr[k] * gr[i - k]
                two += xi[k] * gi[i - k]
                three += xt[k] * gt[i - k]
            ys[i, re, :] = one - two
            ys[i, im, :] = three - (one + two)

    for i in range(n):
        conv = jnp.dot(inv_ref[...], ys[i].astype(BF16), preferred_element_type=F32)
        mix = in_ref[i, 2].astype(F32) * (conv + skip_ref[...] * in_ref[i, 0].astype(F32))
        chunk, place = places[i]
        mixes[chunk][place] = mix.astype(BF16)


def convolve(packed, skip, places):
    n, _, block, chans = packed.shape
    forward, inverse = tables(block)
    return pl.pallas_call(
        lambda *refs: conv_kernel(places, *refs),
        out_shape=[jax.ShapeDtypeStruct((n // 2, block, chans), BF16)] * 2,
        scratch_shapes=[pltpu.VMEM((n, 2 * block, chans), F32)] * 3,
        compiler_params=pltpu.CompilerParams(vmem_limit_bytes=16 * MIB),
        cost_estimate=pl.CostEstimate(flops=2**31, bytes_accessed=4 * MIB, transcendentals=0),
        name="convolve",
    )(packed, skip, jnp.asarray(forward), jnp.asarray(inverse))


def project_kernel(counts, last, here_ref, *refs):
    refs = list(refs[len(counts) :])
    totals = []
    for count in counts:
        pieces, slabs = refs[:count], refs[count : 2 * count]
        del refs[: 2 * count]
        total = refs.pop(0)[...] if last else None
        for piece, slab in zip(pieces, slabs):
            parts, chans, columns = piece.shape[0], slab.shape[2], slab.shape[3]
            left = jnp.concatenate([piece[b] for b in range(parts)], axis=1)
            right = slab[...].reshape(parts * chans, columns)
            term = jnp.dot(left, right, preferred_element_type=F32)
            total = term if total is None else total + term
        totals.append(total)
    if last:
        totals = [total.astype(BF16) for total in totals]

        @pl.when(lax.rem(here_ref[0], 2) == 0)
        def _():
            refs[0][...], refs[1][...] = totals

        @pl.when(lax.rem(here_ref[0], 2) == 1)
        def _():
            refs[1][...], refs[0][...] = totals
    else:
        for ref, total in zip(refs, totals):
            ref[...] = total


def project(chunks, owners, sums, here, weights):
    _, block, chans = chunks[0][0].shape
    m, _, _, columns = weights.shape
    last = sums is not None
    tables, operands, specs = [], [], []
    whole = pl.BlockSpec((m, block, chans), lambda t, *_: (0, 0, 0))
    flat = pl.BlockSpec((block, columns), lambda t, *_: (0, 0))
    for h, pieces in enumerate(chunks):
        tables.append(jnp.asarray(owners[h].reshape(-1)))
        operands += pieces + [weights] * len(pieces)
        specs += [whole] * len(pieces)
        for s in range(len(pieces)):

            def rows(t, here, *tables, h=h, s=s, count=len(pieces)):
                return (0, tables[h][here[0] * count + s], 0, 0)

            specs.append(pl.BlockSpec((m, 1, chans, columns), rows))
        if last:
            operands.append(sums[h])
            specs.append(flat)
    counts = [len(pieces) for pieces in chunks]
    return pl.pallas_call(
        lambda *refs: project_kernel(counts, last, *refs),
        grid_spec=pltpu.PrefetchScalarGridSpec(
            num_scalar_prefetch=1 + len(chunks),
            grid=(1,),
            in_specs=specs,
            out_specs=[flat] * len(chunks),
        ),
        out_shape=[jax.ShapeDtypeStruct((block, columns), BF16 if last else F32)] * len(chunks),
        compiler_params=pltpu.CompilerParams(vmem_limit_bytes=60 * MIB),
        cost_estimate=pl.CostEstimate(flops=0, bytes_accessed=0, transcendentals=0),
        name="project_last" if last else "project_first",
    )(here, *tables, *operands)


def ring_of(deep, across):
    walk = []
    for a in range(across):
        column = list(range(1, deep))
        walk += [d * across + a for d in (column if a % 2 == 0 else column[::-1])]
    return walk + [a for a in reversed(range(across))]


def per_device(outer_gate, inner_gate, values_in, filters, skip_gain, w_out):
    n, m = lax.axis_size("ctx"), lax.axis_size("ch")
    j, k = lax.axis_index("ctx"), lax.axis_index("ch")
    block, wide = outer_gate.shape
    chans = wide // n
    across = n // 4
    half = m // 2
    assert n == 2 * m
    here = jnp.stack([j, k]).astype(jnp.int32)

    def row_block(h, d):
        return (h + 2 * (d % 2)) * across + d // 2

    places = {row_block(h, d): (h, d) for h in range(2) for d in range(m)}

    weights = lax.all_gather(w_out, "ch", axis=0, tiled=True).reshape(m, n, chans, -1)
    packed = pack(outer_gate, inner_gate, values_in, filters, n)
    packed = lax.all_to_all(packed, "ctx", 0, 0)
    skip = lax.dynamic_slice_in_dim(skip_gain, j * chans, chans, 0)[None, :]
    mixes = convolve(packed, skip, places)
    mixes = [lax.all_to_all(mix, "ch", 0, 0) for mix in mixes]

    ring = ring_of(4, across)
    spot = np.argsort(np.array(ring))
    onward = [(ring[p], ring[(p + 1) % n]) for p in range(n)]
    back = [(b, a) for a, b in onward]

    hops = [(n // 2, n // 2 - 1), (n // 2 - 1, n // 2)]
    pieces = [[mix] for mix in mixes]
    offsets = [[0], [0]]
    tips = [[mix, mix] for mix in mixes]
    late = []
    sums = None
    for s in range(n // 2):
        if s >= 2:
            ahead = late[s - 1]
            if s == n // 2 - 1:
                early = 2 * s - 1
                sums = project(
                    [p[:early] for p in pieces],
                    [np.array([[ring[(spot[a] + o) % n] for o in off[:early]] for a in range(n)], np.int32) for off in offsets],
                    None,
                    here,
                    weights,
                )
                ahead = [*ahead, *sums]
            tied = lax.optimization_barrier((*tips[0], *ahead))
            tips[0] = list(tied[:2])
        late.append(list(tips[1]))
        for h in range(2):
            for way, route in enumerate((onward, back)):
                if s < hops[h][way]:
                    tips[h][way] = lax.ppermute(tips[h][way], "ctx", route)
                    pieces[h].append(tips[h][way])
                    offsets[h].append(-(s + 1) if way == 0 else s + 1)

    sent = project(
        [p[early:] for p in pieces],
        [np.array([[ring[(spot[a] + o) % n] for o in off[early:]] for a in range(n)], np.int32) for off in offsets],
        sums,
        here,
        weights,
    )

    found = []
    for e in range(2):
        route = []
        for a in range(n):
            for b in range(m):
                route.append((a * m + b, row_block((a + e) % 2, b) * m + a // 2))
        found.append(lax.ppermute(sent[e], ("ctx", "ch"), route))
    even = (j // across) % 2 == 0
    return jnp.where(even, jnp.concatenate(found, axis=1), jnp.concatenate(found[::-1], axis=1))


def solution(mesh):
    placed = (
        P("ctx", "ch"),
        P("ctx", "ch"),
        P("ctx", "ch"),
        P("ctx", "ch"),
        P("ch"),
        P("ch", "ctx"),
    )
    return jax.shard_map(
        per_device, mesh=mesh, in_specs=placed, out_specs=P("ctx", "ch"), check_vma=False
    )
```

```python
import math

import jax
import jax.numpy as jnp
import numpy as np
from jax import lax
from jax.experimental import pallas as pl
from jax.experimental.pallas import tpu as pltpu
from jax.sharding import PartitionSpec as P

BF16, F32 = jnp.bfloat16, jnp.float32
MIB = 2**20


def tables(block):
    freqs = np.arange(block, dtype=np.float64)[:, None] + 0.5
    window = np.arange(-block, block, dtype=np.float64)[None, :]
    angles = math.pi / block * freqs * window
    forward = np.concatenate([np.cos(angles), -np.sin(angles)], axis=0)
    places = angles[:, block:].T
    inverse = np.concatenate([np.cos(places), -np.sin(places)], axis=1) / block
    return forward.astype(BF16), inverse.astype(BF16)


def pack_kernel(outer_ref, inner_ref, values_ref, filters_ref, out_ref):
    n, _, _, chans = out_ref.shape
    gated = (inner_ref[...].astype(F32) * values_ref[...].astype(F32)).astype(BF16)
    lags = filters_ref[...].astype(BF16)
    outer = outer_ref[...]
    for d in range(n):
        part = slice(d * chans, (d + 1) * chans)
        out_ref[d, 0] = gated[:, part]
        out_ref[d, 1] = lags[:, part]
        out_ref[d, 2] = outer[:, part]


def pack(outer_gate, inner_gate, values_in, filters, n):
    block, wide = outer_gate.shape
    tile = block // 2
    return pl.pallas_call(
        pack_kernel,
        grid=(block // tile,),
        in_specs=[pl.BlockSpec((tile, wide), lambda t: (t, 0))] * 4,
        out_specs=pl.BlockSpec((n, 3, tile, wide // n), lambda t: (0, 0, t, 0)),
        out_shape=jax.ShapeDtypeStruct((n, 3, block, wide // n), BF16),
        compiler_params=pltpu.CompilerParams(vmem_limit_bytes=60 * MIB),
        cost_estimate=pl.CostEstimate(flops=2**18, bytes_accessed=4 * MIB, transcendentals=0),
        name="pack",
    )(outer_gate, inner_gate, values_in, filters)


def conv_kernel(places, in_ref, skip_ref, fwd_ref, inv_ref, mix_ref, xs, gs, ys):
    n, _, block, chans = in_ref.shape
    for k in range(n):
        xs[k] = jnp.dot(fwd_ref[:, block:], in_ref[k, 0], preferred_element_type=F32)
        lag = jnp.dot(fwd_ref[:, block:], in_ref[k, 1], preferred_element_type=F32)
        if k:
            lag += jnp.dot(fwd_ref[:, :block], in_ref[k - 1, 1], preferred_element_type=F32)
        gs[k] = lag

    step = 8

    @pl.loop(0, block // step)
    def _(c):
        re = pl.ds(pl.multiple_of(c * step, step), step)
        im = pl.ds(pl.multiple_of(block + c * step, step), step)
        xr = [xs[k, re, :] for k in range(n)]
        xi = [xs[k, im, :] for k in range(n)]
        gr = [gs[k, re, :] for k in range(n)]
        gi = [gs[k, im, :] for k in range(n)]
        xt = [a + b for a, b in zip(xr, xi)]
        gt = [a + b for a, b in zip(gr, gi)]
        for i in range(n):
            one = xr[0] * gr[i]
            two = xi[0] * gi[i]
            three = xt[0] * gt[i]
            for k in range(1, i + 1):
                one += xr[k] * gr[i - k]
                two += xi[k] * gi[i - k]
                three += xt[k] * gt[i - k]
            ys[i, re, :] = one - two
            ys[i, im, :] = three - (one + two)

    for i in range(n):
        conv = jnp.dot(inv_ref[...], ys[i].astype(BF16), preferred_element_type=F32)
        mix = in_ref[i, 2].astype(F32) * (conv + skip_ref[...] * in_ref[i, 0].astype(F32))
        chunk, place = places[i]
        mix_ref[place, chunk] = mix.astype(BF16)


def convolve(packed, skip, places):
    n, _, block, chans = packed.shape
    forward, inverse = tables(block)
    return pl.pallas_call(
        lambda *refs: conv_kernel(places, *refs),
        out_shape=jax.ShapeDtypeStruct((n // 2, 2, block, chans), BF16),
        scratch_shapes=[pltpu.VMEM((n, 2 * block, chans), F32)] * 3,
        compiler_params=pltpu.CompilerParams(vmem_limit_bytes=16 * MIB),
        cost_estimate=pl.CostEstimate(flops=2**31, bytes_accessed=4 * MIB, transcendentals=0),
        name="convolve",
    )(packed, skip, jnp.asarray(forward), jnp.asarray(inverse))


def project_kernel(shape, m, last, here_ref, table_ref, *refs):
    refs = list(refs)
    total = refs.pop(0)[...] if len(refs) > sum(shape) + m * len(shape) + 1 + last else None
    for parts in shape:
        piece, slabs = refs[:parts], refs[parts : parts + m]
        del refs[: parts + m]
        left, right = [], []
        for b in range(m):
            source = lax.bitwise_xor(here_ref[1], b)
            share = m // parts
            inner = lax.bitwise_and(source, share - 1)
            rows = piece[0][inner]
            if parts == 2:
                rows = jnp.where(source < share, rows, piece[1][inner])
            left.append(rows.reshape(-1, rows.shape[-1]))
            right.append(slabs[b][0])
        term = jnp.dot(
            jnp.concatenate(left, axis=1),
            jnp.concatenate(right, axis=0),
            preferred_element_type=F32,
        )
        total = term if total is None else total + term
    if last:
        total = total.astype(BF16)
        block = total.shape[0] // 2
        chunks = [total[:block], total[block:]]

        @pl.when(lax.rem(here_ref[0], 2) == 0)
        def _():
            refs[0][...], refs[1][...] = chunks

        @pl.when(lax.rem(here_ref[0], 2) == 1)
        def _():
            refs[1][...], refs[0][...] = chunks
    else:
        refs[0][...] = total


def project(pieces, owners, total, here, weights, last=False):
    m = len(weights)
    _, chans, columns = weights[0].shape
    block = pieces[0][0].shape[-2]
    operands, specs = [], []

    def whole(shape):
        return pl.BlockSpec(shape, lambda t, *_: (0,) * len(shape))

    if total is not None:
        operands.append(total)
        specs.append(whole(total.shape))
    for s, piece in enumerate(pieces):
        operands += piece + weights
        specs += [whole(part.shape) for part in piece]

        def rows(t, here, table, s=s):
            return (table[here[0] * len(pieces) + s], 0, 0)

        specs += [pl.BlockSpec((1, chans, columns), rows)] * m
    outs = [((block, columns), BF16)] * 2 if last else [((2 * block, columns), F32)]
    shape = [len(piece) for piece in pieces]
    return pl.pallas_call(
        lambda *refs: project_kernel(shape, m, last, *refs),
        grid_spec=pltpu.PrefetchScalarGridSpec(
            num_scalar_prefetch=2,
            grid=(1,),
            in_specs=specs,
            out_specs=[whole(size) for size, _ in outs],
        ),
        out_shape=[jax.ShapeDtypeStruct(*out) for out in outs],
        compiler_params=pltpu.CompilerParams(vmem_limit_bytes=60 * MIB),
        cost_estimate=pl.CostEstimate(flops=0, bytes_accessed=0, transcendentals=0),
        name="project",
    )(here, jnp.asarray(owners.reshape(-1)), *operands)


def ring_of(deep, across):
    walk = []
    for a in range(across):
        column = list(range(1, deep))
        walk += [d * across + a for d in (column if a % 2 == 0 else column[::-1])]
    return walk + [a for a in reversed(range(across))]


def per_device(outer_gate, inner_gate, values_in, filters, skip_gain, w_out):
    n, m = lax.axis_size("ctx"), lax.axis_size("ch")
    j, k = lax.axis_index("ctx"), lax.axis_index("ch")
    block, wide = outer_gate.shape
    chans = wide // n
    across = n // 4
    half = m // 2
    assert n == 2 * m
    here = jnp.stack([j, k]).astype(jnp.int32)

    def row_block(h, d):
        return (h + 2 * (d % 2)) * across + d // 2

    places = {row_block(h, d): (h, d) for h in range(2) for d in range(m)}

    weights = [w_out.reshape(n, chans, -1)]
    while len(weights) < m:
        pairs = [(d, d ^ len(weights)) for d in range(m)]
        if len(weights) == 1:
            weights.append(lax.ppermute(weights[0], "ch", pairs))
        else:
            for even in list(weights[::2]):
                far = lax.ppermute(even, "ch", pairs)
                weights += [far, lax.ppermute(far, "ch", [(d, d ^ 1) for d in range(m)])]

    packed = pack(outer_gate, inner_gate, values_in, filters, n)
    packed = lax.all_to_all(packed, "ctx", 0, 0)
    skip = lax.dynamic_slice_in_dim(skip_gain, j * chans, chans, 0)[None, :]
    packed, weights = lax.optimization_barrier((packed, weights))
    mix = lax.all_to_all(convolve(packed, skip, places), "ch", 0, 0)

    ring = ring_of(4, across)
    spot = np.argsort(np.array(ring))
    routes = [[(ring[p], ring[(p + way) % n]) for p in range(n)] for way in (1, -1)]

    def owners(offsets):
        return np.array([[ring[(spot[a] + o) % n] for o in offsets] for a in range(n)], np.int32)

    tips = [mix, mix]
    pieces, offsets = [[mix]], [0]
    for s in range(1, n // 2):
        if s == n // 2 - 1:
            total = project(pieces, owners(offsets), None, here, weights)
        tips = [lax.ppermute(tip, "ctx", route) for tip, route in zip(tips, routes)]
        pieces += [[tip] for tip in tips]
        offsets += [-s, s]
    tips, total = lax.optimization_barrier((tips, total))
    halves = [lax.ppermute(tip[way * half : (way + 1) * half], "ctx", routes[way]) for way, tip in enumerate(tips)]
    total = project([[tip] for tip in tips], owners(offsets[-2:]), total[0], here, weights)
    sent = project([halves], owners([n // 2]), total[0], here, weights, last=True)

    found = []
    for e in range(2):
        route = []
        for a in range(n):
            for b in range(m):
                route.append((a * m + b, row_block((a + e) % 2, b) * m + a // 2))
        found.append(lax.ppermute(sent[e], ("ctx", "ch"), route))
    even = (j // across) % 2 == 0
    return jnp.where(even, jnp.concatenate(found, axis=1), jnp.concatenate(found[::-1], axis=1))


def solution(mesh):
    placed = (
        P("ctx", "ch"),
        P("ctx", "ch"),
        P("ctx", "ch"),
        P("ctx", "ch"),
        P("ch"),
        P("ch", "ctx"),
    )
    return jax.shard_map(
        per_device, mesh=mesh, in_specs=placed, out_specs=P("ctx", "ch"), check_vma=False
    )
```

```python
import math

import jax
import jax.numpy as jnp
import numpy as np
from jax import lax
from jax.experimental import pallas as pl
from jax.experimental.pallas import tpu as pltpu
from jax.sharding import PartitionSpec as P

BF16, F32 = jnp.bfloat16, jnp.float32
MIB = 2**20


def tables(block):
    freqs = np.arange(block, dtype=np.float64)[:, None] + 0.5
    window = np.arange(-block, block, dtype=np.float64)[None, :]
    angles = math.pi / block * freqs * window
    forward = np.concatenate([np.cos(angles), -np.sin(angles)], axis=0)
    places = angles[:, block:].T
    inverse = np.concatenate([np.cos(places), -np.sin(places)], axis=1) / block
    return forward.astype(BF16), inverse.astype(BF16)


def pack_kernel(outer_ref, inner_ref, values_ref, filters_ref, out_ref):
    n, _, _, chans = out_ref.shape
    gated = (inner_ref[...].astype(F32) * values_ref[...].astype(F32)).astype(BF16)
    lags = filters_ref[...].astype(BF16)
    outer = outer_ref[...]
    for d in range(n):
        part = slice(d * chans, (d + 1) * chans)
        out_ref[d, 0] = gated[:, part]
        out_ref[d, 1] = lags[:, part]
        out_ref[d, 2] = outer[:, part]


def pack(outer_gate, inner_gate, values_in, filters, n):
    block, wide = outer_gate.shape
    tile = block // 2
    return pl.pallas_call(
        pack_kernel,
        grid=(block // tile,),
        in_specs=[pl.BlockSpec((tile, wide), lambda t: (t, 0))] * 4,
        out_specs=pl.BlockSpec((n, 3, tile, wide // n), lambda t: (0, 0, t, 0)),
        out_shape=jax.ShapeDtypeStruct((n, 3, block, wide // n), BF16),
        compiler_params=pltpu.CompilerParams(vmem_limit_bytes=60 * MIB),
        cost_estimate=pl.CostEstimate(flops=2**18, bytes_accessed=4 * MIB, transcendentals=0),
        name="pack",
    )(outer_gate, inner_gate, values_in, filters)


def conv_kernel(places, here_ref, in_ref, skip_ref, fwd_ref, inv_ref, *rest):
    mixes, (xs, gs, ys, mix_ref) = rest[:-4], rest[-4:]
    n, _, block, chans = in_ref.shape
    for k in range(n):
        xs[k] = jnp.dot(fwd_ref[:, block:], in_ref[k, 0], preferred_element_type=F32)
        lag = jnp.dot(fwd_ref[:, block:], in_ref[k, 1], preferred_element_type=F32)
        if k:
            lag += jnp.dot(fwd_ref[:, :block], in_ref[k - 1, 1], preferred_element_type=F32)
        gs[k] = lag

    step = 8

    @pl.loop(0, block // step)
    def _(c):
        re = pl.ds(pl.multiple_of(c * step, step), step)
        im = pl.ds(pl.multiple_of(block + c * step, step), step)
        xr = [xs[k, re, :] for k in range(n)]
        xi = [xs[k, im, :] for k in range(n)]
        gr = [gs[k, re, :] for k in range(n)]
        gi = [gs[k, im, :] for k in range(n)]
        xt = [a + b for a, b in zip(xr, xi)]
        gt = [a + b for a, b in zip(gr, gi)]
        for i in range(n):
            one = xr[0] * gr[i]
            two = xi[0] * gi[i]
            three = xt[0] * gt[i]
            for k in range(1, i + 1):
                one += xr[k] * gr[i - k]
                two += xi[k] * gi[i - k]
                three += xt[k] * gt[i - k]
            ys[i, re, :] = one - two
            ys[i, im, :] = three - (one + two)

    for i in range(n):
        conv = jnp.dot(inv_ref[...], ys[i].astype(BF16), preferred_element_type=F32)
        mix = in_ref[i, 2].astype(F32) * (conv + skip_ref[...] * in_ref[i, 0].astype(F32))
        chunk, place = places[i]
        mix_ref[place, chunk] = mix.astype(BF16)
    for b, ref in enumerate(mixes):
        ref[...] = mix_ref[lax.bitwise_xor(here_ref[1], b)]


def convolve(here, packed, skip, places):
    n, _, block, chans = packed.shape
    m = n // 2
    forward, inverse = tables(block)

    def whole(*shape):
        return pl.BlockSpec(shape, lambda t, here: (0,) * len(shape))

    return pl.pallas_call(
        lambda *refs: conv_kernel(places, *refs),
        grid_spec=pltpu.PrefetchScalarGridSpec(
            num_scalar_prefetch=1,
            grid=(1,),
            in_specs=[whole(*a.shape) for a in (packed, skip, forward, inverse)],
            out_specs=[whole(2, block, chans)] * m,
            scratch_shapes=[pltpu.VMEM((n, 2 * block, chans), F32)] * 3
            + [pltpu.VMEM((m, 2, block, chans), BF16)],
        ),
        out_shape=[jax.ShapeDtypeStruct((2, block, chans), BF16)] * m,
        compiler_params=pltpu.CompilerParams(vmem_limit_bytes=20 * MIB),
        cost_estimate=pl.CostEstimate(flops=2**31, bytes_accessed=4 * MIB, transcendentals=0),
        name="convolve",
    )(here, packed, skip, jnp.asarray(forward), jnp.asarray(inverse))


def project_kernel(count, m, last, here_ref, table_ref, *refs):
    refs = list(refs)
    total = refs.pop(0)[...] if len(refs) > (2 + m) * count + 1 + last else None
    for _ in range(count):
        piece, slabs = refs[:2], refs[2 : 2 + m]
        del refs[: 2 + m]
        share = m // 2
        left = [piece[b // share][b % share] for b in range(m)]
        term = jnp.dot(
            jnp.concatenate([a.reshape(-1, a.shape[-1]) for a in left], axis=1),
            jnp.concatenate([slab[0] for slab in slabs], axis=0),
            preferred_element_type=F32,
        )
        total = term if total is None else total + term
    if last:
        total = total.astype(BF16)
        block = total.shape[0] // 2
        chunks = [total[:block], total[block:]]

        @pl.when(lax.rem(here_ref[0], 2) == 0)
        def _():
            refs[0][...], refs[1][...] = chunks

        @pl.when(lax.rem(here_ref[0], 2) == 1)
        def _():
            refs[1][...], refs[0][...] = chunks
    else:
        refs[0][...] = total


def project(pieces, owners, total, here, weights, last=False):
    m, count = len(weights), len(pieces)
    _, chans, columns = weights[0].shape
    block = pieces[0][0].shape[-2]
    operands, specs = [], []

    def whole(shape):
        return pl.BlockSpec(shape, lambda t, *_: (0,) * len(shape))

    if total is not None:
        operands.append(total)
        specs.append(whole(total.shape))
    for s, piece in enumerate(pieces):
        operands += list(piece) + weights
        specs += [whole(part.shape) for part in piece]

        def rows(t, here, table, s=s):
            return (table[here[0] * count + s], 0, 0)

        specs += [pl.BlockSpec((1, chans, columns), rows)] * m
    outs = [((block, columns), BF16)] * 2 if last else [((2 * block, columns), F32)]
    found = pl.pallas_call(
        lambda *refs: project_kernel(count, m, last, *refs),
        grid_spec=pltpu.PrefetchScalarGridSpec(
            num_scalar_prefetch=2,
            grid=(1,),
            in_specs=specs,
            out_specs=[whole(size) for size, _ in outs],
        ),
        out_shape=[jax.ShapeDtypeStruct(*out) for out in outs],
        compiler_params=pltpu.CompilerParams(vmem_limit_bytes=60 * MIB),
        cost_estimate=pl.CostEstimate(flops=0, bytes_accessed=0, transcendentals=0),
        name="project",
    )(here, jnp.asarray(owners.reshape(-1)), *operands)
    return found if last else found[0]


def ring_of(deep, across):
    walk = []
    for a in range(across):
        column = list(range(1, deep))
        walk += [d * across + a for d in (column if a % 2 == 0 else column[::-1])]
    return walk + [a for a in reversed(range(across))]


def per_device(outer_gate, inner_gate, values_in, filters, skip_gain, w_out):
    n, m = lax.axis_size("ctx"), lax.axis_size("ch")
    j, k = lax.axis_index("ctx"), lax.axis_index("ch")
    block, wide = outer_gate.shape
    chans = wide // n
    across = n // 4
    half = m // 2
    assert n == 2 * m
    here = jnp.stack([j, k]).astype(jnp.int32)

    def row_block(h, d):
        return (h + 2 * (d % 2)) * across + d // 2

    places = {row_block(h, d): (h, d) for h in range(2) for d in range(m)}

    weights = [w_out.reshape(n, chans, -1)]
    while len(weights) < m:
        pairs = [(d, d ^ len(weights)) for d in range(m)]
        if len(weights) == 1:
            weights.append(lax.ppermute(weights[0], "ch", pairs))
        else:
            for even in list(weights[::2]):
                far = lax.ppermute(even, "ch", pairs)
                weights += [far, lax.ppermute(far, "ch", [(d, d ^ 1) for d in range(m)])]

    packed = pack(outer_gate, inner_gate, values_in, filters, n)
    packed = lax.all_to_all(packed, "ctx", 0, 0)
    skip = lax.dynamic_slice_in_dim(skip_gain, j * chans, chans, 0)[None, :]
    packed, weights = lax.optimization_barrier((packed, weights))
    parts = list(convolve(here, packed, skip, places))
    parts = parts[:1] + [
        lax.ppermute(part, "ch", [(d, d ^ b) for d in range(m)]) for b, part in enumerate(parts) if b
    ]

    ring = ring_of(4, across)
    spot = np.argsort(np.array(ring))
    routes = [[(ring[p], ring[(p + way) % n]) for p in range(n)] for way in (1, -1)]

    def owners(*offsets):
        return np.array([[ring[(spot[a] + o) % n] for o in offsets] for a in range(n)], np.int32)

    own = [jnp.stack(parts[:half]), jnp.stack(parts[half:])]
    tips = [[piece, piece] for piece in own]
    arrived, sums = [([own], [0])], None
    for s in range(1, n // 2 + 1):
        if s >= 3:
            ready = arrived[: s - 1] if s == 3 else arrived[s - 2 : s - 1]
            pieces, offsets = (sum(lists, []) for lists in zip(*ready))
            sums = project(pieces, owners(*offsets), sums, here, weights)
            tips[0], sums = lax.optimization_barrier((tips[0], sums))
        for h in range(2):
            for way in range(2) if s < n // 2 else [h]:
                tips[h][way] = lax.ppermute(tips[h][way], "ctx", routes[way])
        if s < n // 2:
            arrived.append(([list(piece) for piece in zip(*tips)], [-s, s]))
    pieces, offsets = arrived[-1]
    sums = project(pieces, owners(*offsets), sums, here, weights)
    sent = project([[tips[0][0], tips[1][1]]], owners(n // 2), sums, here, weights, last=True)

    found = []
    for e in range(2):
        route = []
        for a in range(n):
            for b in range(m):
                route.append((a * m + b, row_block((a + e) % 2, b) * m + a // 2))
        found.append(lax.ppermute(sent[e], ("ctx", "ch"), route))
    even = (j // across) % 2 == 0
    return jnp.where(even, jnp.concatenate(found, axis=1), jnp.concatenate(found[::-1], axis=1))


def solution(mesh):
    placed = (
        P("ctx", "ch"),
        P("ctx", "ch"),
        P("ctx", "ch"),
        P("ctx", "ch"),
        P("ch"),
        P("ch", "ctx"),
    )
    return jax.shard_map(
        per_device, mesh=mesh, in_specs=placed, out_specs=P("ctx", "ch"), check_vma=False
    )
```

```python
import math

import jax
import jax.numpy as jnp
import numpy as np
from jax import lax
from jax.experimental import pallas as pl
from jax.experimental.pallas import tpu as pltpu
from jax.sharding import PartitionSpec as P

BF16, F32 = jnp.bfloat16, jnp.float32
MIB = 2**20


def tables(block):
    freqs = np.arange(block, dtype=np.float64)[:, None] + 0.5
    window = np.arange(-block, block, dtype=np.float64)[None, :]
    angles = math.pi / block * freqs * window
    forward = np.concatenate([np.cos(angles), -np.sin(angles)], axis=0)
    places = angles[:, block:].T
    inverse = np.concatenate([np.cos(places), -np.sin(places)], axis=1) / block
    return forward.astype(BF16), inverse.astype(BF16)


def pack_kernel(outer_ref, inner_ref, values_ref, filters_ref, out_ref):
    n, _, _, chans = out_ref.shape
    gated = (inner_ref[...].astype(F32) * values_ref[...].astype(F32)).astype(BF16)
    lags = filters_ref[...].astype(BF16)
    outer = outer_ref[...]
    for d in range(n):
        part = slice(d * chans, (d + 1) * chans)
        out_ref[d, 0] = gated[:, part]
        out_ref[d, 1] = lags[:, part]
        out_ref[d, 2] = outer[:, part]


def pack(outer_gate, inner_gate, values_in, filters, n):
    block, wide = outer_gate.shape
    tile = block // 2
    return pl.pallas_call(
        pack_kernel,
        grid=(block // tile,),
        in_specs=[pl.BlockSpec((tile, wide), lambda t: (t, 0))] * 4,
        out_specs=pl.BlockSpec((n, 3, tile, wide // n), lambda t: (0, 0, t, 0)),
        out_shape=jax.ShapeDtypeStruct((n, 3, block, wide // n), BF16),
        compiler_params=pltpu.CompilerParams(vmem_limit_bytes=60 * MIB),
        cost_estimate=pl.CostEstimate(flops=2**18, bytes_accessed=4 * MIB, transcendentals=0),
        name="pack",
    )(outer_gate, inner_gate, values_in, filters)


def row_block(side, k, m):
    return 2 * ((k & 1) * (m // 2) + (k >> 1)) + side


def conv_kernel(here_ref, in_ref, skip_ref, fwd_ref, inv_ref, *rest):
    mixes, (xs, gs, ys, mix_ref) = rest[:-4], rest[-4:]
    n, _, block, chans = in_ref.shape
    for k in range(n):
        xs[k] = jnp.dot(fwd_ref[:, block:], in_ref[k, 0], preferred_element_type=F32)
        lag = jnp.dot(fwd_ref[:, block:], in_ref[k, 1], preferred_element_type=F32)
        if k:
            lag += jnp.dot(fwd_ref[:, :block], in_ref[k - 1, 1], preferred_element_type=F32)
        gs[k] = lag

    step = 8

    @pl.loop(0, block // step)
    def _(c):
        re = pl.ds(pl.multiple_of(c * step, step), step)
        im = pl.ds(pl.multiple_of(block + c * step, step), step)
        xr = [xs[k, re, :] for k in range(n)]
        xi = [xs[k, im, :] for k in range(n)]
        gr = [gs[k, re, :] for k in range(n)]
        gi = [gs[k, im, :] for k in range(n)]
        xt = [a + b for a, b in zip(xr, xi)]
        gt = [a + b for a, b in zip(gr, gi)]
        for i in range(n):
            one = xr[0] * gr[i]
            two = xi[0] * gi[i]
            three = xt[0] * gt[i]
            for k in range(1, i + 1):
                one += xr[k] * gr[i - k]
                two += xi[k] * gi[i - k]
                three += xt[k] * gt[i - k]
            ys[i, re, :] = one - two
            ys[i, im, :] = three - (one + two)

    for i in range(n):
        conv = jnp.dot(inv_ref[...], ys[i].astype(BF16), preferred_element_type=F32)
        mix = in_ref[i, 2].astype(F32) * (conv + skip_ref[...] * in_ref[i, 0].astype(F32))
        mix_ref[i] = mix.astype(BF16)
    m = n // 2
    for s, ref in enumerate(mixes):
        side = lax.bitwise_xor(lax.bitwise_and(here_ref[0], 1), s // m)
        ref[...] = mix_ref[row_block(side, lax.bitwise_xor(here_ref[1], s % m), m)]


def convolve(here, packed, skip):
    n, _, block, chans = packed.shape
    forward, inverse = tables(block)

    def whole(*shape):
        return pl.BlockSpec(shape, lambda t, here: (0,) * len(shape))

    return pl.pallas_call(
        conv_kernel,
        grid_spec=pltpu.PrefetchScalarGridSpec(
            num_scalar_prefetch=1,
            grid=(1,),
            in_specs=[whole(*a.shape) for a in (packed, skip, forward, inverse)],
            out_specs=[whole(block, chans)] * n,
            scratch_shapes=[pltpu.VMEM((n, 2 * block, chans), F32)] * 3
            + [pltpu.VMEM((n, block, chans), BF16)],
        ),
        out_shape=[jax.ShapeDtypeStruct((block, chans), BF16)] * n,
        compiler_params=pltpu.CompilerParams(vmem_limit_bytes=20 * MIB),
        cost_estimate=pl.CostEstimate(flops=2**31, bytes_accessed=4 * MIB, transcendentals=0),
        name="convolve",
    )(here, packed, skip, jnp.asarray(forward), jnp.asarray(inverse))


def project_kernel(count, n, last, here_ref, table_ref, *refs):
    refs = list(refs)
    total = None
    if len(refs) > (2 + n) * count + 1:
        earlier = refs.pop(0)
        total = [earlier[0], earlier[1]]
    side = lax.bitwise_and(here_ref[0], 1)
    m = n // 2
    for _ in range(count):
        piece, slabs = refs[:2], refs[2 : 2 + n]
        del refs[: 2 + n]
        left = jnp.concatenate([piece[s // m][s % m] for s in range(n)], axis=1)
        for half in range(2):
            right = [slabs[half * m + s % m][lax.bitwise_xor(side, s // m)] for s in range(n)]
            term = jnp.dot(left, jnp.concatenate(right, axis=0), preferred_element_type=F32)
            if total is None or len(total) <= half:
                total = (total or []) + [term]
            else:
                total[half] += term
    out = refs[0]
    columns = total[0].shape[1]
    if last:

        @pl.when(side == 0)
        def _():
            for half in range(2):
                out[:, half * columns : (half + 1) * columns] = total[half].astype(BF16)

        @pl.when(side == 1)
        def _():
            for half in range(2):
                out[:, (1 - half) * columns : (2 - half) * columns] = total[half].astype(BF16)
    else:
        for half in range(2):
            out[half] = total[half]


def project(pieces, owners, total, here, weights, last=False):
    n, count = len(weights), len(pieces)
    _, chans, columns = weights[0].shape
    block = pieces[0][0].shape[-2]
    operands, specs = [], []

    def whole(shape):
        return pl.BlockSpec(shape, lambda t, *_: (0,) * len(shape))

    if total is not None:
        operands.append(total)
        specs.append(whole(total.shape))
    for s, piece in enumerate(pieces):
        operands += list(piece) + weights
        specs += [whole(part.shape) for part in piece]

        def rows(t, here, table, s=s):
            return (table[here[0] * count + s], 0, 0)

        specs += [pl.BlockSpec((2, chans, columns), rows)] * n
    size, kind = ((block, 2 * columns), BF16) if last else ((2, block, columns), F32)
    return pl.pallas_call(
        lambda *refs: project_kernel(count, n, last, *refs),
        grid_spec=pltpu.PrefetchScalarGridSpec(
            num_scalar_prefetch=2,
            grid=(1,),
            in_specs=specs,
            out_specs=whole(size),
        ),
        out_shape=jax.ShapeDtypeStruct(size, kind),
        compiler_params=pltpu.CompilerParams(vmem_limit_bytes=60 * MIB),
        cost_estimate=pl.CostEstimate(flops=0, bytes_accessed=0, transcendentals=0),
        name="project",
    )(here, jnp.asarray(owners.reshape(-1)), *operands)


def ring_of(count):
    if count == 4:
        return [0, 2, 3, 1]
    walk = []
    across = count // 4
    for a in range(across):
        column = list(range(1, 4))
        walk += [d * across + a for d in (column if a % 2 == 0 else column[::-1])]
    return walk + [a for a in reversed(range(across))]


def per_device(outer_gate, inner_gate, values_in, filters, skip_gain, w_out):
    n, m = lax.axis_size("ctx"), lax.axis_size("ch")
    j, k = lax.axis_index("ctx"), lax.axis_index("ch")
    block, wide = outer_gate.shape
    chans = wide // n
    assert n == 2 * m
    here = jnp.stack([j, k]).astype(jnp.int32)

    def plane_swap(a, b):
        return [(i * m + d, (i ^ a) * m + (d ^ b)) for i in range(n) for d in range(m)]

    mine = w_out.reshape(n, chans, -1)
    over = lax.ppermute(mine, ("ctx", "ch"), plane_swap(1, 0))
    sides = [[mine], [over]]
    for part in sides:
        bit = 1
        while bit < m:
            if bit == 1:
                part.append(lax.ppermute(part[0], "ch", [(d, d ^ 1) for d in range(m)]))
            else:
                for even in list(part[::2]):
                    far = lax.ppermute(even, "ch", [(d, d ^ bit) for d in range(m)])
                    part += [far, lax.ppermute(far, "ch", [(d, d ^ 1) for d in range(m)])]
            bit *= 2
    weights = sides[0] + sides[1]

    packed = pack(outer_gate, inner_gate, values_in, filters, n)
    packed = lax.all_to_all(packed, "ctx", 0, 0)
    skip = lax.dynamic_slice_in_dim(skip_gain, j * chans, chans, 0)[None, :]
    packed, near, over = lax.optimization_barrier((packed, sides[0], over))
    parts = list(convolve(here, packed, skip))
    parts = parts[:1] + [
        lax.ppermute(part, ("ctx", "ch"), plane_swap(s // m, s % m)) for s, part in enumerate(parts) if s
    ]

    ring = ring_of(m)
    spot = np.argsort(np.array(ring))
    routes = [
        [(2 * ring[p] + side, 2 * ring[(p + way) % m] + side) for p in range(m) for side in range(2)]
        for way in (1, -1)
    ]

    def owners(*offsets):
        return np.array([[ring[(spot[a // 2] + o) % m] for o in offsets] for a in range(n)], np.int32)

    own = [jnp.stack(parts[:m]), jnp.stack(parts[m:])]
    tips = [[piece, piece] for piece in own]
    arrived, sums = [([own], [0])], None
    for s in range(1, m // 2 + 1):
        if s >= 2:
            pieces, offsets = arrived[s - 2]
            sums = project(pieces, owners(*offsets), sums, here, weights)
            tips[0], sums = lax.optimization_barrier((tips[0], sums))
        for h in range(2):
            for way in range(2) if s < m // 2 else [h]:
                tips[h][way] = lax.ppermute(tips[h][way], "ctx", routes[way])
        if s < m // 2:
            arrived.append(([list(piece) for piece in zip(*tips)], [-s, s]))
    pieces, offsets = arrived[-1]
    sums = project(pieces, owners(*offsets), sums, here, weights)
    mixed = project([[tips[0][0], tips[1][1]]], owners(m // 2), sums, here, weights, last=True)

    route = [(i * m + d, row_block(i % 2, d, m) * m + i // 2) for i in range(n) for d in range(m)]
    return lax.ppermute(mixed, ("ctx", "ch"), route)


def solution(mesh):
    placed = (
        P("ctx", "ch"),
        P("ctx", "ch"),
        P("ctx", "ch"),
        P("ctx", "ch"),
        P("ch"),
        P("ch", "ctx"),
    )
    return jax.shard_map(
        per_device, mesh=mesh, in_specs=placed, out_specs=P("ctx", "ch"), check_vma=False
    )
```

```python
import math

import jax
import jax.numpy as jnp
import numpy as np
from jax import lax
from jax.experimental import pallas as pl
from jax.experimental.pallas import tpu as pltpu
from jax.sharding import PartitionSpec as P

BF16, F32 = jnp.bfloat16, jnp.float32
MIB = 2**20


def tables(block):
    freqs = np.arange(block, dtype=np.float64)[:, None] + 0.5
    window = np.arange(-block, block, dtype=np.float64)[None, :]
    angles = math.pi / block * freqs * window
    forward = np.concatenate([np.cos(angles), -np.sin(angles)], axis=0)
    places = angles[:, block:].T
    inverse = np.concatenate([np.cos(places), -np.sin(places)], axis=1) / block
    return forward.astype(BF16), inverse.astype(BF16)


def pack_kernel(here_ref, outer_ref, inner_ref, values_ref, filters_ref, *rest):
    outs, ordered = rest[:-1], rest[-1]
    n, _, _, chans = ordered.shape
    gated = (inner_ref[...].astype(F32) * values_ref[...].astype(F32)).astype(BF16)
    lags = filters_ref[...].astype(BF16)
    outer = outer_ref[...]
    for d in range(n):
        part = slice(d * chans, (d + 1) * chans)
        ordered[d, 0] = gated[:, part]
        ordered[d, 1] = lags[:, part]
        ordered[d, 2] = outer[:, part]
    for d, out in enumerate(outs):
        out[...] = ordered[lax.bitwise_xor(here_ref[0], d)]


def pack(here, outer_gate, inner_gate, values_in, filters, n):
    block, wide = outer_gate.shape
    tile, chans = block // 2, wide // n
    return pl.pallas_call(
        pack_kernel,
        grid_spec=pltpu.PrefetchScalarGridSpec(
            num_scalar_prefetch=1,
            grid=(block // tile,),
            in_specs=[pl.BlockSpec((tile, wide), lambda t, here: (t, 0))] * 4,
            out_specs=[pl.BlockSpec((3, tile, chans), lambda t, here: (0, t, 0))] * n,
            scratch_shapes=[pltpu.VMEM((n, 3, tile, chans), BF16)],
        ),
        out_shape=[jax.ShapeDtypeStruct((3, block, chans), BF16)] * n,
        compiler_params=pltpu.CompilerParams(vmem_limit_bytes=60 * MIB),
        cost_estimate=pl.CostEstimate(flops=0, bytes_accessed=0, transcendentals=0),
        name="pack",
    )(here, outer_gate, inner_gate, values_in, filters)


def conv_kernel(places, here_ref, skip_ref, fwd_ref, inv_ref, *rest):
    rest, (xs, gs, ys, mix_ref, in_ref) = rest[:-5], rest[-5:]
    n, _, block, chans = in_ref.shape
    mixes = rest[n:]
    for d, ref in enumerate(rest[:n]):
        in_ref[lax.bitwise_xor(here_ref[0], d)] = ref[...]
    for k in range(n):
        xs[k] = jnp.dot(fwd_ref[:, block:], in_ref[k, 0], preferred_element_type=F32)
        lag = jnp.dot(fwd_ref[:, block:], in_ref[k, 1], preferred_element_type=F32)
        if k:
            lag += jnp.dot(fwd_ref[:, :block], in_ref[k - 1, 1], preferred_element_type=F32)
        gs[k] = lag

    step = 8

    @pl.loop(0, block // step)
    def _(c):
        re = pl.ds(pl.multiple_of(c * step, step), step)
        im = pl.ds(pl.multiple_of(block + c * step, step), step)
        xr = [xs[k, re, :] for k in range(n)]
        xi = [xs[k, im, :] for k in range(n)]
        gr = [gs[k, re, :] for k in range(n)]
        gi = [gs[k, im, :] for k in range(n)]
        xt = [a + b for a, b in zip(xr, xi)]
        gt = [a + b for a, b in zip(gr, gi)]
        for i in range(n):
            one = xr[0] * gr[i]
            two = xi[0] * gi[i]
            three = xt[0] * gt[i]
            for k in range(1, i + 1):
                one += xr[k] * gr[i - k]
                two += xi[k] * gi[i - k]
                three += xt[k] * gt[i - k]
            ys[i, re, :] = one - two
            ys[i, im, :] = three - (one + two)

    for i in range(n):
        conv = jnp.dot(inv_ref[...], ys[i].astype(BF16), preferred_element_type=F32)
        mix = in_ref[i, 2].astype(F32) * (conv + skip_ref[...] * in_ref[i, 0].astype(F32))
        chunk, place = places[i]
        mix_ref[place, chunk] = mix.astype(BF16)
    for b, ref in enumerate(mixes):
        ref[...] = mix_ref[lax.bitwise_xor(here_ref[1], b)]


def convolve(here, packed, skip, places):
    n = len(packed)
    _, block, chans = packed[0].shape
    m = n // 2
    forward, inverse = tables(block)

    def whole(*shape):
        return pl.BlockSpec(shape, lambda t, here: (0,) * len(shape))

    return pl.pallas_call(
        lambda *refs: conv_kernel(places, *refs),
        grid_spec=pltpu.PrefetchScalarGridSpec(
            num_scalar_prefetch=1,
            grid=(1,),
            in_specs=[whole(*a.shape) for a in (skip, forward, inverse, *packed)],
            out_specs=[whole(2, block, chans)] * m,
            scratch_shapes=[pltpu.VMEM((n, 2 * block, chans), F32)] * 3
            + [pltpu.VMEM((m, 2, block, chans), BF16), pltpu.VMEM((n, 3, block, chans), BF16)],
        ),
        out_shape=[jax.ShapeDtypeStruct((2, block, chans), BF16)] * m,
        compiler_params=pltpu.CompilerParams(vmem_limit_bytes=20 * MIB),
        cost_estimate=pl.CostEstimate(flops=2**31, bytes_accessed=4 * MIB, transcendentals=0),
        name="convolve",
    )(here, skip, jnp.asarray(forward), jnp.asarray(inverse), *packed)


def project_kernel(count, m, last, here_ref, table_ref, *refs):
    refs = list(refs)
    total = refs.pop(0)[...] if len(refs) > (2 + m) * count + 1 + last else None
    for _ in range(count):
        piece, slabs = refs[:2], refs[2 : 2 + m]
        del refs[: 2 + m]
        share = m // 2
        left = [piece[b // share][b % share] for b in range(m)]
        term = jnp.dot(
            jnp.concatenate([a.reshape(-1, a.shape[-1]) for a in left], axis=1),
            jnp.concatenate([slab[0] for slab in slabs], axis=0),
            preferred_element_type=F32,
        )
        total = term if total is None else total + term
    if last:
        total = total.astype(BF16)
        block = total.shape[0] // 2
        chunks = [total[:block], total[block:]]

        @pl.when(lax.rem(here_ref[0], 2) == 0)
        def _():
            refs[0][...], refs[1][...] = chunks

        @pl.when(lax.rem(here_ref[0], 2) == 1)
        def _():
            refs[1][...], refs[0][...] = chunks
    else:
        refs[0][...] = total


def project(pieces, owners, total, here, weights, last=False):
    m, count = len(weights), len(pieces)
    _, chans, columns = weights[0].shape
    block = pieces[0][0].shape[-2]
    operands, specs = [], []

    def whole(shape):
        return pl.BlockSpec(shape, lambda t, *_: (0,) * len(shape))

    if total is not None:
        operands.append(total)
        specs.append(whole(total.shape))
    for s, piece in enumerate(pieces):
        operands += list(piece) + weights
        specs += [whole(part.shape) for part in piece]

        def rows(t, here, table, s=s):
            return (table[here[0] * count + s], 0, 0)

        specs += [pl.BlockSpec((1, chans, columns), rows)] * m
    outs = [((block, columns), BF16)] * 2 if last else [((2 * block, columns), F32)]
    found = pl.pallas_call(
        lambda *refs: project_kernel(count, m, last, *refs),
        grid_spec=pltpu.PrefetchScalarGridSpec(
            num_scalar_prefetch=2,
            grid=(1,),
            in_specs=specs,
            out_specs=[whole(size) for size, _ in outs],
        ),
        out_shape=[jax.ShapeDtypeStruct(*out) for out in outs],
        compiler_params=pltpu.CompilerParams(vmem_limit_bytes=(10 if last else 60) * MIB),
        cost_estimate=pl.CostEstimate(flops=0, bytes_accessed=0, transcendentals=0),
        name="project",
    )(here, jnp.asarray(owners.reshape(-1)), *operands)
    return found if last else found[0]


def ring_of(deep, across):
    walk = []
    for a in range(across):
        column = list(range(1, deep))
        walk += [d * across + a for d in (column if a % 2 == 0 else column[::-1])]
    return walk + [a for a in reversed(range(across))]


def per_device(outer_gate, inner_gate, values_in, filters, skip_gain, w_out):
    n, m = lax.axis_size("ctx"), lax.axis_size("ch")
    j, k = lax.axis_index("ctx"), lax.axis_index("ch")
    block, wide = outer_gate.shape
    chans = wide // n
    across = n // 4
    half = m // 2
    assert n == 2 * m
    here = jnp.stack([j, k]).astype(jnp.int32)

    def row_block(h, d):
        return (h + 2 * (d % 2)) * across + d // 2

    places = {row_block(h, d): (h, d) for h in range(2) for d in range(m)}

    packed = list(pack(here, outer_gate, inner_gate, values_in, filters, n))
    far, near = list(range(n - 1, n // 2 - 1, -1)), list(range(1, n // 2))
    order = far[:1] + [d for pair in zip(far[1:], near) for d in pair]
    for d in order:
        packed[d] = lax.ppermute(packed[d], "ctx", [(i, i ^ d) for i in range(n)])
    skip = lax.dynamic_slice_in_dim(skip_gain, j * chans, chans, 0)[None, :]

    weights = [w_out.reshape(n, chans, -1)]
    for b in range(1, m):
        weights.append(lax.ppermute(weights[0], "ch", [(d, d ^ b) for d in range(m)]))
    packed, weights[:-1] = lax.optimization_barrier((packed, weights[:-1]))
    parts = list(convolve(here, packed, skip, places))
    parts = parts[:1] + [
        lax.ppermute(part, "ch", [(d, d ^ b) for d in range(m)]) for b, part in enumerate(parts) if b
    ]

    ring = ring_of(4, across)
    spot = np.argsort(np.array(ring))
    routes = [[(ring[p], ring[(p + way) % n]) for p in range(n)] for way in (1, -1)]

    def owners(*offsets):
        return np.array([[ring[(spot[a] + o) % n] for o in offsets] for a in range(n)], np.int32)

    parts[half:], weights[-1] = lax.optimization_barrier((parts[half:], weights[-1]))
    own = [jnp.stack(parts[:half]), jnp.stack(parts[half:])]
    tips = [[piece, piece] for piece in own]
    arrived, sums = [([own], [0])], None
    for s in range(1, n // 2 + 1):
        if s >= 3:
            ready = arrived[: s - 1] if s == 3 else arrived[s - 2 : s - 1]
            pieces, offsets = (sum(lists, []) for lists in zip(*ready))
            sums = project(pieces, owners(*offsets), sums, here, weights)
            tips[0], sums = lax.optimization_barrier((tips[0], sums))
        for h in range(2):
            for way in range(2) if s < n // 2 else [h]:
                tips[h][way] = lax.ppermute(tips[h][way], "ctx", routes[way])
        if s < n // 2:
            arrived.append(([list(piece) for piece in zip(*tips)], [-s, s]))
    pieces, offsets = arrived[-1]
    sums = project(pieces, owners(*offsets), sums, here, weights)
    sent = project([[tips[0][0], tips[1][1]]], owners(n // 2), sums, here, weights, last=True)

    found = []
    for e in range(2):
        route = []
        for a in range(n):
            for b in range(m):
                route.append((a * m + b, row_block((a + e) % 2, b) * m + a // 2))
        found.append(lax.ppermute(sent[e], ("ctx", "ch"), route))
    even = (j // across) % 2 == 0
    return jnp.where(even, jnp.concatenate(found, axis=1), jnp.concatenate(found[::-1], axis=1))


def solution(mesh):
    placed = (
        P("ctx", "ch"),
        P("ctx", "ch"),
        P("ctx", "ch"),
        P("ctx", "ch"),
        P("ch"),
        P("ch", "ctx"),
    )
    return jax.shard_map(
        per_device, mesh=mesh, in_specs=placed, out_specs=P("ctx", "ch"), check_vma=False
    )
```

```python
import math

import jax
import jax.numpy as jnp
import numpy as np
from jax import lax
from jax.experimental import pallas as pl
from jax.experimental.pallas import tpu as pltpu
from jax.sharding import PartitionSpec as P

BF16, F32 = jnp.bfloat16, jnp.float32
MIB = 2**20


def tables(block):
    freqs = np.arange(block, dtype=np.float64)[:, None] + 0.5
    window = np.arange(-block, block, dtype=np.float64)[None, :]
    angles = math.pi / block * freqs * window
    forward = np.concatenate([np.cos(angles), -np.sin(angles)], axis=0)
    places = angles[:, block:].T
    inverse = np.concatenate([np.cos(places), -np.sin(places)], axis=1) / block
    return forward.astype(BF16), inverse.astype(BF16)


def pack_kernel(outer_ref, inner_ref, values_ref, filters_ref, out_ref):
    n, _, _, chans = out_ref.shape
    gated = (inner_ref[...].astype(F32) * values_ref[...].astype(F32)).astype(BF16)
    lags = filters_ref[...].astype(BF16)
    outer = outer_ref[...]
    for d in range(n):
        part = slice(d * chans, (d + 1) * chans)
        out_ref[d, 0] = gated[:, part]
        out_ref[d, 1] = lags[:, part]
        out_ref[d, 2] = outer[:, part]


def pack(outer_gate, inner_gate, values_in, filters, n):
    block, wide = outer_gate.shape
    tile = block // 4
    return pl.pallas_call(
        pack_kernel,
        grid=(block // tile,),
        in_specs=[pl.BlockSpec((tile, wide), lambda t: (t, 0))] * 4,
        out_specs=pl.BlockSpec((n, 3, tile, wide // n), lambda t: (0, 0, t, 0)),
        out_shape=jax.ShapeDtypeStruct((n, 3, block, wide // n), BF16),
        compiler_params=pltpu.CompilerParams(vmem_limit_bytes=60 * MIB),
        cost_estimate=pl.CostEstimate(flops=2**18, bytes_accessed=4 * MIB, transcendentals=0),
        name="pack",
    )(outer_gate, inner_gate, values_in, filters)


def conv_kernel(places, here_ref, in_ref, skip_ref, fwd_ref, inv_ref, *rest):
    mixes, (xs, gs, ys, mix_ref) = rest[:-4], rest[-4:]
    n, _, block, chans = in_ref.shape
    empty = jnp.zeros((block, chans), BF16)
    for k in range(0, n, 2):
        pair = jnp.concatenate([in_ref[k, 0], in_ref[k + 1, 0]], axis=1)
        both = jnp.dot(fwd_ref[:, block:], pair, preferred_element_type=F32)
        xs[k], xs[k + 1] = both[:, :chans], both[:, chans:]
        pair = jnp.concatenate([in_ref[k, 1], in_ref[k + 1, 1]], axis=1)
        both = jnp.dot(fwd_ref[:, block:], pair, preferred_element_type=F32)
        pair = jnp.concatenate([in_ref[k - 1, 1] if k else empty, in_ref[k, 1]], axis=1)
        both += jnp.dot(fwd_ref[:, :block], pair, preferred_element_type=F32)
        gs[k], gs[k + 1] = both[:, :chans], both[:, chans:]

    step = 8

    @pl.loop(0, block // step)
    def _(c):
        re = pl.ds(pl.multiple_of(c * step, step), step)
        im = pl.ds(pl.multiple_of(block + c * step, step), step)
        xr = [xs[k, re, :] for k in range(n)]
        xi = [xs[k, im, :] for k in range(n)]
        gr = [gs[k, re, :] for k in range(n)]
        gi = [gs[k, im, :] for k in range(n)]
        xt = [a + b for a, b in zip(xr, xi)]
        gt = [a + b for a, b in zip(gr, gi)]
        for i in range(n):
            one = xr[0] * gr[i]
            two = xi[0] * gi[i]
            three = xt[0] * gt[i]
            for k in range(1, i + 1):
                one += xr[k] * gr[i - k]
                two += xi[k] * gi[i - k]
                three += xt[k] * gt[i - k]
            ys[i, re, :] = one - two
            ys[i, im, :] = three - (one + two)

    for k in range(0, n, 2):
        pair = jnp.concatenate([ys[k].astype(BF16), ys[k + 1].astype(BF16)], axis=1)
        both = jnp.dot(inv_ref[...], pair, preferred_element_type=F32)
        for i, conv in ((k, both[:, :chans]), (k + 1, both[:, chans:])):
            mix = in_ref[i, 2].astype(F32) * (conv + skip_ref[...] * in_ref[i, 0].astype(F32))
            chunk, place = places[i]
            mix_ref[place, chunk] = mix.astype(BF16)
    for b, ref in enumerate(mixes):
        ref[...] = mix_ref[lax.bitwise_xor(here_ref[1], b)]


def convolve(here, packed, skip, places):
    n, _, block, chans = packed.shape
    m = n // 2
    forward, inverse = tables(block)

    def whole(*shape):
        return pl.BlockSpec(shape, lambda t, here: (0,) * len(shape))

    return pl.pallas_call(
        lambda *refs: conv_kernel(places, *refs),
        grid_spec=pltpu.PrefetchScalarGridSpec(
            num_scalar_prefetch=1,
            grid=(1,),
            in_specs=[whole(*a.shape) for a in (packed, skip, forward, inverse)],
            out_specs=[whole(2, block, chans)] * m,
            scratch_shapes=[pltpu.VMEM((n, 2 * block, chans), F32)] * 3
            + [pltpu.VMEM((m, 2, block, chans), BF16)],
        ),
        out_shape=[jax.ShapeDtypeStruct((2, block, chans), BF16)] * m,
        compiler_params=pltpu.CompilerParams(vmem_limit_bytes=20 * MIB),
        cost_estimate=pl.CostEstimate(flops=2**31, bytes_accessed=4 * MIB, transcendentals=0),
        name="convolve",
    )(here, packed, skip, jnp.asarray(forward), jnp.asarray(inverse))


def project_kernel(count, m, here_ref, table_ref, *refs):
    refs = list(refs)
    total = refs.pop(0)[...] if len(refs) > (2 + m) * count + 1 else None
    for _ in range(count):
        piece, slabs = refs[:2], refs[2 : 2 + m]
        del refs[: 2 + m]
        share = m // 2
        left = [piece[b // share][b % share] for b in range(m)]
        term = jnp.dot(
            jnp.concatenate([a.reshape(-1, a.shape[-1]) for a in left], axis=1),
            jnp.concatenate([slab[0] for slab in slabs], axis=0),
            preferred_element_type=F32,
        )
        total = term if total is None else total + term
    refs[0][...] = total.astype(refs[0].dtype)


def project(pieces, owners, total, here, weights, turn=None):
    m, count = len(weights), len(pieces)
    _, chans, columns = weights[0].shape
    block = pieces[0][0].shape[-2]
    operands, specs = [], []
    rows, kind = (2 * block, F32) if turn is None else (block, BF16)

    def chunk(here):
        return 0 if turn is None else lax.rem(here[0] + turn, 2)

    if total is not None:
        operands.append(total)
        specs.append(pl.BlockSpec((rows, columns), lambda t, here, _: (chunk(here), 0)))
    for s, piece in enumerate(pieces):
        operands += list(piece) + weights
        share = (m // 2, rows // block, block, chans)
        specs += [pl.BlockSpec(share, lambda t, here, _: (0, chunk(here), 0, 0))] * 2

        def slab(t, here, table, s=s):
            return (table[here[0] * count + s], 0, 0)

        specs += [pl.BlockSpec((1, chans, columns), slab)] * m
    return pl.pallas_call(
        lambda *refs: project_kernel(count, m, *refs),
        grid_spec=pltpu.PrefetchScalarGridSpec(
            num_scalar_prefetch=2,
            grid=(1,),
            in_specs=specs,
            out_specs=pl.BlockSpec((rows, columns), lambda t, *_: (0, 0)),
        ),
        out_shape=jax.ShapeDtypeStruct((rows, columns), kind),
        compiler_params=pltpu.CompilerParams(vmem_limit_bytes=60 * MIB),
        cost_estimate=pl.CostEstimate(flops=0, bytes_accessed=0, transcendentals=0),
        name="project",
    )(here, jnp.asarray(owners.reshape(-1)), *operands)


def ring_of(deep, across):
    walk = []
    for a in range(across):
        column = list(range(1, deep))
        walk += [d * across + a for d in (column if a % 2 == 0 else column[::-1])]
    return walk + [a for a in reversed(range(across))]


def per_device(outer_gate, inner_gate, values_in, filters, skip_gain, w_out):
    n, m = lax.axis_size("ctx"), lax.axis_size("ch")
    j, k = lax.axis_index("ctx"), lax.axis_index("ch")
    block, wide = outer_gate.shape
    chans = wide // n
    across = n // 4
    half = m // 2
    assert n == 2 * m
    here = jnp.stack([j, k]).astype(jnp.int32)

    def row_block(h, d):
        return (h + 2 * (d % 2)) * across + d // 2

    places = {row_block(h, d): (h, d) for h in range(2) for d in range(m)}

    weights = [w_out.reshape(n, chans, -1)]
    while len(weights) < m:
        pairs = [(d, d ^ len(weights)) for d in range(m)]
        if len(weights) == 1:
            weights.append(lax.ppermute(weights[0], "ch", pairs))
        else:
            for even in list(weights[::2]):
                far = lax.ppermute(even, "ch", pairs)
                weights += [far, lax.ppermute(far, "ch", [(d, d ^ 1) for d in range(m)])]

    packed = pack(outer_gate, inner_gate, values_in, filters, n)
    packed = lax.all_to_all(packed, "ctx", 0, 0)
    skip = lax.dynamic_slice_in_dim(skip_gain, j * chans, chans, 0)[None, :]
    packed, weights = lax.optimization_barrier((packed, weights))
    parts = list(convolve(here, packed, skip, places))
    parts = parts[:1] + [
        lax.ppermute(part, "ch", [(d, d ^ b) for d in range(m)]) for b, part in enumerate(parts) if b
    ]

    ring = ring_of(4, across)
    spot = np.argsort(np.array(ring))
    routes = [[(ring[p], ring[(p + way) % n]) for p in range(n)] for way in (1, -1)]

    def owners(*offsets):
        return np.array([[ring[(spot[a] + o) % n] for o in offsets] for a in range(n)], np.int32)

    own = [jnp.stack(parts[:half]), jnp.stack(parts[half:])]
    tips = [[piece, piece] for piece in own]
    arrived, sums = [([own], [0])], None
    for s in range(1, n // 2 + 1):
        if s >= 3:
            ready = arrived[: s - 1] if s == 3 else arrived[s - 2 : s - 1]
            pieces, offsets = (sum(lists, []) for lists in zip(*ready))
            sums = project(pieces, owners(*offsets), sums, here, weights)
            tips[0], sums = lax.optimization_barrier((tips[0], sums))
        for h in range(2):
            for way in range(2) if s < n // 2 else [h]:
                tips[h][way] = lax.ppermute(tips[h][way], "ctx", routes[way])
        if s < n // 2:
            arrived.append(([list(piece) for piece in zip(*tips)], [-s, s]))
    pieces, offsets = arrived[-1]
    sums = project(pieces, owners(*offsets), sums, here, weights)
    last = [[tips[0][0], tips[1][1]]]
    sent = [project(last, owners(n // 2), sums, here, weights, turn) for turn in range(2)]

    found = []
    for e in range(2):
        route = []
        for a in range(n):
            for b in range(m):
                route.append((a * m + b, row_block((a + e) % 2, b) * m + a // 2))
        found.append(lax.ppermute(sent[e], ("ctx", "ch"), route))
    even = (j // across) % 2 == 0
    return jnp.where(even, jnp.concatenate(found, axis=1), jnp.concatenate(found[::-1], axis=1))


def solution(mesh):
    placed = (
        P("ctx", "ch"),
        P("ctx", "ch"),
        P("ctx", "ch"),
        P("ctx", "ch"),
        P("ch"),
        P("ch", "ctx"),
    )
    return jax.shard_map(
        per_device, mesh=mesh, in_specs=placed, out_specs=P("ctx", "ch"), check_vma=False
    )
```

```python
import math

import jax
import jax.numpy as jnp
import numpy as np
from jax import lax
from jax.experimental import pallas as pl
from jax.experimental.pallas import tpu as pltpu
from jax.sharding import PartitionSpec as P

BF16, F32 = jnp.bfloat16, jnp.float32
MIB = 2**20


def tables(block):
    freqs = np.arange(block, dtype=np.float64)[:, None] + 0.5
    window = np.arange(-block, block, dtype=np.float64)[None, :]
    angles = math.pi / block * freqs * window
    forward = np.concatenate([np.cos(angles), -np.sin(angles)], axis=0)
    places = angles[:, block:].T
    inverse = np.concatenate([np.cos(places), -np.sin(places)], axis=1) / block
    return forward.astype(BF16), inverse.astype(BF16)


def pack_kernel(outer_ref, inner_ref, values_ref, filters_ref, out_ref):
    n, _, _, chans = out_ref.shape
    gated = (inner_ref[...].astype(F32) * values_ref[...].astype(F32)).astype(BF16)
    lags = filters_ref[...].astype(BF16)
    outer = outer_ref[...]
    for d in range(n):
        part = slice(d * chans, (d + 1) * chans)
        out_ref[d, 0] = gated[:, part]
        out_ref[d, 1] = lags[:, part]
        out_ref[d, 2] = outer[:, part]


def pack(outer_gate, inner_gate, values_in, filters, n):
    block, wide = outer_gate.shape
    tile = block // 2
    return pl.pallas_call(
        pack_kernel,
        grid=(block // tile,),
        in_specs=[pl.BlockSpec((tile, wide), lambda t: (t, 0))] * 4,
        out_specs=pl.BlockSpec((n, 3, tile, wide // n), lambda t: (0, 0, t, 0)),
        out_shape=jax.ShapeDtypeStruct((n, 3, block, wide // n), BF16),
        compiler_params=pltpu.CompilerParams(vmem_limit_bytes=60 * MIB),
        cost_estimate=pl.CostEstimate(flops=2**18, bytes_accessed=4 * MIB, transcendentals=0),
        name="pack",
    )(outer_gate, inner_gate, values_in, filters)


def conv_kernel(places, here_ref, in_ref, skip_ref, fwd_ref, inv_ref, *rest):
    mixes, (xs, gs, ys, mix_ref) = rest[:-4], rest[-4:]
    n, _, block, chans = in_ref.shape
    empty = jnp.zeros((block, chans), BF16)
    for k in range(0, n, 2):
        pair = jnp.concatenate([in_ref[k, 0], in_ref[k + 1, 0]], axis=1)
        both = jnp.dot(fwd_ref[:, block:], pair, preferred_element_type=F32)
        xs[k], xs[k + 1] = both[:, :chans], both[:, chans:]
        pair = jnp.concatenate([in_ref[k, 1], in_ref[k + 1, 1]], axis=1)
        both = jnp.dot(fwd_ref[:, block:], pair, preferred_element_type=F32)
        pair = jnp.concatenate([in_ref[k - 1, 1] if k else empty, in_ref[k, 1]], axis=1)
        both += jnp.dot(fwd_ref[:, :block], pair, preferred_element_type=F32)
        gs[k], gs[k + 1] = both[:, :chans], both[:, chans:]

    step = 8

    @pl.loop(0, block // step)
    def _(c):
        re = pl.ds(pl.multiple_of(c * step, step), step)
        im = pl.ds(pl.multiple_of(block + c * step, step), step)
        xr = [xs[k, re, :] for k in range(n)]
        xi = [xs[k, im, :] for k in range(n)]
        gr = [gs[k, re, :] for k in range(n)]
        gi = [gs[k, im, :] for k in range(n)]
        xt = [a + b for a, b in zip(xr, xi)]
        gt = [a + b for a, b in zip(gr, gi)]
        for i in range(n):
            one = xr[0] * gr[i]
            two = xi[0] * gi[i]
            three = xt[0] * gt[i]
            for k in range(1, i + 1):
                one += xr[k] * gr[i - k]
                two += xi[k] * gi[i - k]
                three += xt[k] * gt[i - k]
            ys[i, re, :] = one - two
            ys[i, im, :] = three - (one + two)

    for k in range(0, n, 2):
        pair = jnp.concatenate([ys[k].astype(BF16), ys[k + 1].astype(BF16)], axis=1)
        both = jnp.dot(inv_ref[...], pair, preferred_element_type=F32)
        for i, conv in ((k, both[:, :chans]), (k + 1, both[:, chans:])):
            mix = in_ref[i, 2].astype(F32) * (conv + skip_ref[...] * in_ref[i, 0].astype(F32))
            chunk, place = places[i]
            mix_ref[place, chunk] = mix.astype(BF16)
    for b, ref in enumerate(mixes):
        ref[...] = mix_ref[lax.bitwise_xor(here_ref[1], b)]


def convolve(here, packed, skip, places):
    n, _, block, chans = packed.shape
    m = n // 2
    forward, inverse = tables(block)

    def whole(*shape):
        return pl.BlockSpec(shape, lambda t, here: (0,) * len(shape))

    return pl.pallas_call(
        lambda *refs: conv_kernel(places, *refs),
        grid_spec=pltpu.PrefetchScalarGridSpec(
            num_scalar_prefetch=1,
            grid=(1,),
            in_specs=[whole(*a.shape) for a in (packed, skip, forward, inverse)],
            out_specs=[whole(2, block, chans)] * m,
            scratch_shapes=[pltpu.VMEM((n, 2 * block, chans), F32)] * 3
            + [pltpu.VMEM((m, 2, block, chans), BF16)],
        ),
        out_shape=[jax.ShapeDtypeStruct((2, block, chans), BF16)] * m,
        compiler_params=pltpu.CompilerParams(vmem_limit_bytes=20 * MIB),
        cost_estimate=pl.CostEstimate(flops=2**31, bytes_accessed=4 * MIB, transcendentals=0),
        name="convolve",
    )(here, packed, skip, jnp.asarray(forward), jnp.asarray(inverse))


def project_kernel(count, m, last, here_ref, table_ref, *refs):
    refs = list(refs)
    total = refs.pop(0)[...] if len(refs) > (2 + m) * count + 1 + last else None
    for _ in range(count):
        piece, slabs = refs[:2], refs[2 : 2 + m]
        del refs[: 2 + m]
        share = m // 2
        left = [piece[b // share][b % share] for b in range(m)]
        term = jnp.dot(
            jnp.concatenate([a.reshape(-1, a.shape[-1]) for a in left], axis=1),
            jnp.concatenate([slab[0] for slab in slabs], axis=0),
            preferred_element_type=F32,
        )
        total = term if total is None else total + term
    if last:
        total = total.astype(BF16)
        block = total.shape[0] // 2
        chunks = [total[:block], total[block:]]

        @pl.when(lax.rem(here_ref[0], 2) == 0)
        def _():
            refs[0][...], refs[1][...] = chunks

        @pl.when(lax.rem(here_ref[0], 2) == 1)
        def _():
            refs[1][...], refs[0][...] = chunks
    else:
        refs[0][...] = total


def project(pieces, owners, total, here, weights, last=False, grant=60):
    m, count = len(weights), len(pieces)
    _, chans, columns = weights[0].shape
    block = pieces[0][0].shape[-2]
    operands, specs = [], []

    def whole(shape):
        return pl.BlockSpec(shape, lambda t, *_: (0,) * len(shape))

    if total is not None:
        operands.append(total)
        specs.append(whole(total.shape))
    for s, piece in enumerate(pieces):
        operands += list(piece) + weights
        specs += [whole(part.shape) for part in piece]

        def rows(t, here, table, s=s):
            return (table[here[0] * count + s], 0, 0)

        specs += [pl.BlockSpec((1, chans, columns), rows)] * m
    outs = [((block, columns), BF16)] * 2 if last else [((2 * block, columns), F32)]
    found = pl.pallas_call(
        lambda *refs: project_kernel(count, m, last, *refs),
        grid_spec=pltpu.PrefetchScalarGridSpec(
            num_scalar_prefetch=2,
            grid=(1,),
            in_specs=specs,
            out_specs=[whole(size) for size, _ in outs],
        ),
        out_shape=[jax.ShapeDtypeStruct(*out) for out in outs],
        compiler_params=pltpu.CompilerParams(vmem_limit_bytes=grant * MIB),
        cost_estimate=pl.CostEstimate(flops=0, bytes_accessed=0, transcendentals=0),
        name="project",
    )(here, jnp.asarray(owners.reshape(-1)), *operands)
    return found if last else found[0]


def ring_of(deep, across):
    walk = []
    for a in range(across):
        column = list(range(1, deep))
        walk += [d * across + a for d in (column if a % 2 == 0 else column[::-1])]
    return walk + [a for a in reversed(range(across))]


def per_device(outer_gate, inner_gate, values_in, filters, skip_gain, w_out):
    n, m = lax.axis_size("ctx"), lax.axis_size("ch")
    j, k = lax.axis_index("ctx"), lax.axis_index("ch")
    block, wide = outer_gate.shape
    chans = wide // n
    across = n // 4
    half = m // 2
    assert n == 2 * m
    here = jnp.stack([j, k]).astype(jnp.int32)

    def row_block(h, d):
        return (h + 2 * (d % 2)) * across + d // 2

    places = {row_block(h, d): (h, d) for h in range(2) for d in range(m)}

    weights = [w_out.reshape(n, chans, -1)]
    while len(weights) < m:
        pairs = [(d, d ^ len(weights)) for d in range(m)]
        if len(weights) == 1:
            weights.append(lax.ppermute(weights[0], "ch", pairs))
        else:
            for even in list(weights[::2]):
                far = lax.ppermute(even, "ch", pairs)
                weights += [far, lax.ppermute(far, "ch", [(d, d ^ 1) for d in range(m)])]

    packed = pack(outer_gate, inner_gate, values_in, filters, n)
    packed = lax.all_to_all(packed, "ctx", 0, 0)
    skip = lax.dynamic_slice_in_dim(skip_gain, j * chans, chans, 0)[None, :]
    packed, weights = lax.optimization_barrier((packed, weights))
    parts = list(convolve(here, packed, skip, places))
    parts = parts[:1] + [
        lax.ppermute(part, "ch", [(d, d ^ b) for d in range(m)]) for b, part in enumerate(parts) if b
    ]

    ring = ring_of(4, across)
    spot = np.argsort(np.array(ring))
    routes = [[(ring[p], ring[(p + way) % n]) for p in range(n)] for way in (1, -1)]

    def owners(*offsets):
        return np.array([[ring[(spot[a] + o) % n] for o in offsets] for a in range(n)], np.int32)

    own = [jnp.stack(parts[:half]), jnp.stack(parts[half:])]
    tips = [[piece, piece] for piece in own]
    arrived, sums = [([own], [0])], None
    for s in range(1, n // 2 + 1):
        if s >= 3:
            ready = arrived[: s - 1] if s == 3 else arrived[s - 2 : s - 1]
            pieces, offsets = (sum(lists, []) for lists in zip(*ready))
            sums = project(pieces, owners(*offsets), sums, here, weights)
            tips[0], sums = lax.optimization_barrier((tips[0], sums))
        for h in range(2):
            for way in range(2) if s < n // 2 else [h]:
                tips[h][way] = lax.ppermute(tips[h][way], "ctx", routes[way])
        if s < n // 2:
            arrived.append(([list(piece) for piece in zip(*tips)], [-s, s]))
    pieces, offsets = arrived[-1]
    sums = project(pieces, owners(*offsets), sums, here, weights, grant=44)
    final = [[tips[0][0], tips[1][1]]]
    sent = project(final, owners(n // 2), sums, here, weights, last=True, grant=44)

    found = []
    for e in range(2):
        route = []
        for a in range(n):
            for b in range(m):
                route.append((a * m + b, row_block((a + e) % 2, b) * m + a // 2))
        found.append(lax.ppermute(sent[e], ("ctx", "ch"), route))
    even = (j // across) % 2 == 0
    return jnp.where(even, jnp.concatenate(found, axis=1), jnp.concatenate(found[::-1], axis=1))


def solution(mesh):
    placed = (
        P("ctx", "ch"),
        P("ctx", "ch"),
        P("ctx", "ch"),
        P("ctx", "ch"),
        P("ch"),
        P("ch", "ctx"),
    )
    return jax.shard_map(
        per_device, mesh=mesh, in_specs=placed, out_specs=P("ctx", "ch"), check_vma=False
    )
```

```python
import math

import jax
import jax.numpy as jnp
import numpy as np
from jax import lax
from jax.experimental import pallas as pl
from jax.experimental.pallas import tpu as pltpu
from jax.sharding import PartitionSpec as P

BF16, F32 = jnp.bfloat16, jnp.float32
MIB = 2**20


def tables(block):
    freqs = np.arange(block, dtype=np.float64)[:, None] + 0.5
    window = np.arange(-block, block, dtype=np.float64)[None, :]
    angles = math.pi / block * freqs * window
    forward = np.concatenate([np.cos(angles), -np.sin(angles)], axis=0)
    places = angles[:, block:].T
    inverse = np.concatenate([np.cos(places), -np.sin(places)], axis=1) / block
    return forward.astype(BF16), inverse.astype(BF16)


def pack_kernel(outer_ref, inner_ref, values_ref, filters_ref, out_ref):
    n, _, _, chans = out_ref.shape
    gated = (inner_ref[...].astype(F32) * values_ref[...].astype(F32)).astype(BF16)
    lags = filters_ref[...].astype(BF16)
    outer = outer_ref[...]
    for d in range(n):
        part = slice(d * chans, (d + 1) * chans)
        out_ref[d, 0] = gated[:, part]
        out_ref[d, 1] = lags[:, part]
        out_ref[d, 2] = outer[:, part]


def pack(outer_gate, inner_gate, values_in, filters, n):
    block, wide = outer_gate.shape
    tile = block // 2
    return pl.pallas_call(
        pack_kernel,
        grid=(block // tile,),
        in_specs=[pl.BlockSpec((tile, wide), lambda t: (t, 0))] * 4,
        out_specs=pl.BlockSpec((n, 3, tile, wide // n), lambda t: (0, 0, t, 0)),
        out_shape=jax.ShapeDtypeStruct((n, 3, block, wide // n), BF16),
        compiler_params=pltpu.CompilerParams(vmem_limit_bytes=60 * MIB),
        cost_estimate=pl.CostEstimate(flops=2**18, bytes_accessed=4 * MIB, transcendentals=0),
        name="pack",
    )(outer_gate, inner_gate, values_in, filters)


def conv_kernel(places, here_ref, in_ref, skip_ref, fwd_ref, inv_ref, *rest):
    mixes, (xs, gs, ys, mix_ref) = rest[:-4], rest[-4:]
    n, _, block, chans = in_ref.shape
    empty = jnp.zeros((block, chans), BF16)
    for k in range(0, n, 2):
        pair = jnp.concatenate([in_ref[k, 0], in_ref[k + 1, 0]], axis=1)
        both = jnp.dot(fwd_ref[:, block:], pair, preferred_element_type=F32)
        xs[k], xs[k + 1] = both[:, :chans], both[:, chans:]
        pair = jnp.concatenate([in_ref[k, 1], in_ref[k + 1, 1]], axis=1)
        both = jnp.dot(fwd_ref[:, block:], pair, preferred_element_type=F32)
        pair = jnp.concatenate([in_ref[k - 1, 1] if k else empty, in_ref[k, 1]], axis=1)
        both += jnp.dot(fwd_ref[:, :block], pair, preferred_element_type=F32)
        gs[k], gs[k + 1] = both[:, :chans], both[:, chans:]

    step = 8

    @pl.loop(0, block // step)
    def _(c):
        re = pl.ds(pl.multiple_of(c * step, step), step)
        im = pl.ds(pl.multiple_of(block + c * step, step), step)
        xr = [xs[k, re, :] for k in range(n)]
        xi = [xs[k, im, :] for k in range(n)]
        gr = [gs[k, re, :] for k in range(n)]
        gi = [gs[k, im, :] for k in range(n)]
        xt = [a + b for a, b in zip(xr, xi)]
        gt = [a + b for a, b in zip(gr, gi)]
        for i in range(n):
            one = xr[0] * gr[i]
            two = xi[0] * gi[i]
            three = xt[0] * gt[i]
            for k in range(1, i + 1):
                one += xr[k] * gr[i - k]
                two += xi[k] * gi[i - k]
                three += xt[k] * gt[i - k]
            ys[i, re, :] = one - two
            ys[i, im, :] = three - (one + two)

    for k in range(0, n, 2):
        pair = jnp.concatenate([ys[k].astype(BF16), ys[k + 1].astype(BF16)], axis=1)
        both = jnp.dot(inv_ref[...], pair, preferred_element_type=F32)
        for i, conv in ((k, both[:, :chans]), (k + 1, both[:, chans:])):
            mix = in_ref[i, 2].astype(F32) * (conv + skip_ref[...] * in_ref[i, 0].astype(F32))
            chunk, place = places[i]
            mix_ref[place, chunk] = mix.astype(BF16)
    for b, ref in enumerate(mixes):
        ref[...] = mix_ref[lax.bitwise_xor(here_ref[1], b)]


def convolve(here, packed, skip, places):
    n, _, block, chans = packed.shape
    m = n // 2
    forward, inverse = tables(block)

    def whole(*shape):
        return pl.BlockSpec(shape, lambda t, here: (0,) * len(shape))

    return pl.pallas_call(
        lambda *refs: conv_kernel(places, *refs),
        grid_spec=pltpu.PrefetchScalarGridSpec(
            num_scalar_prefetch=1,
            grid=(1,),
            in_specs=[whole(*a.shape) for a in (packed, skip, forward, inverse)],
            out_specs=[whole(2, block, chans)] * m,
            scratch_shapes=[pltpu.VMEM((n, 2 * block, chans), F32)] * 3
            + [pltpu.VMEM((m, 2, block, chans), BF16)],
        ),
        out_shape=[jax.ShapeDtypeStruct((2, block, chans), BF16)] * m,
        compiler_params=pltpu.CompilerParams(vmem_limit_bytes=20 * MIB),
        cost_estimate=pl.CostEstimate(flops=2**31, bytes_accessed=4 * MIB, transcendentals=0),
        name="convolve",
    )(here, packed, skip, jnp.asarray(forward), jnp.asarray(inverse))


def project_kernel(count, m, last, here_ref, table_ref, *refs):
    refs = list(refs)
    total = refs.pop(0)[...] if len(refs) > (2 + m) * count + 1 + last else None
    for _ in range(count):
        piece, slabs = refs[:2], refs[2 : 2 + m]
        del refs[: 2 + m]
        share = m // 2
        left = [piece[b // share][b % share] for b in range(m)]
        term = jnp.dot(
            jnp.concatenate([a.reshape(-1, a.shape[-1]) for a in left], axis=1),
            jnp.concatenate([slab[0] for slab in slabs], axis=0),
            preferred_element_type=F32,
        )
        total = term if total is None else total + term
    if last:
        total = total.astype(BF16)
        block = total.shape[0] // 2
        chunks = [total[:block], total[block:]]

        @pl.when(lax.rem(here_ref[0], 2) == 0)
        def _():
            refs[0][...], refs[1][...] = chunks

        @pl.when(lax.rem(here_ref[0], 2) == 1)
        def _():
            refs[1][...], refs[0][...] = chunks
    else:
        refs[0][...] = total


def project(pieces, owners, total, here, weights, last=False, grant=60):
    m, count = len(weights), len(pieces)
    _, chans, columns = weights[0].shape
    block = pieces[0][0].shape[-2]
    operands, specs = [], []

    def whole(shape):
        return pl.BlockSpec(shape, lambda t, *_: (0,) * len(shape))

    if total is not None:
        operands.append(total)
        specs.append(whole(total.shape))
    for s, piece in enumerate(pieces):
        operands += list(piece) + weights
        specs += [whole(part.shape) for part in piece]

        def rows(t, here, table, s=s):
            return (table[here[0] * count + s], 0, 0)

        specs += [pl.BlockSpec((1, chans, columns), rows)] * m
    outs = [((block, columns), BF16)] * 2 if last else [((2 * block, columns), F32)]
    found = pl.pallas_call(
        lambda *refs: project_kernel(count, m, last, *refs),
        grid_spec=pltpu.PrefetchScalarGridSpec(
            num_scalar_prefetch=2,
            grid=(1,),
            in_specs=specs,
            out_specs=[whole(size) for size, _ in outs],
        ),
        out_shape=[jax.ShapeDtypeStruct(*out) for out in outs],
        compiler_params=pltpu.CompilerParams(vmem_limit_bytes=grant * MIB),
        cost_estimate=pl.CostEstimate(flops=0, bytes_accessed=0, transcendentals=0),
        name="project",
    )(here, jnp.asarray(owners.reshape(-1)), *operands)
    return found if last else found[0]


def ring_of(deep, across):
    walk = []
    for a in range(across):
        column = list(range(1, deep))
        walk += [d * across + a for d in (column if a % 2 == 0 else column[::-1])]
    return walk + [a for a in reversed(range(across))]


def per_device(outer_gate, inner_gate, values_in, filters, skip_gain, w_out):
    n, m = lax.axis_size("ctx"), lax.axis_size("ch")
    j, k = lax.axis_index("ctx"), lax.axis_index("ch")
    block, wide = outer_gate.shape
    chans = wide // n
    across = n // 4
    half = m // 2
    assert n == 2 * m
    here = jnp.stack([j, k]).astype(jnp.int32)

    def row_block(h, d):
        return (h + 2 * (d % 2)) * across + d // 2

    places = {row_block(h, d): (h, d) for h in range(2) for d in range(m)}

    weights = [w_out.reshape(n, chans, -1)]
    while len(weights) < m:
        pairs = [(d, d ^ len(weights)) for d in range(m)]
        if len(weights) == 1:
            weights.append(lax.ppermute(weights[0], "ch", pairs))
        else:
            for even in list(weights[::2]):
                far = lax.ppermute(even, "ch", pairs)
                weights += [far, lax.ppermute(far, "ch", [(d, d ^ 1) for d in range(m)])]

    packed = pack(outer_gate, inner_gate, values_in, filters, n)
    packed = lax.all_to_all(packed, "ctx", 0, 0)
    skip = lax.dynamic_slice_in_dim(skip_gain, j * chans, chans, 0)[None, :]
    packed, weights = lax.optimization_barrier((packed, weights))
    parts = list(convolve(here, packed, skip, places))
    parts = parts[:1] + [
        lax.ppermute(part, "ch", [(d, d ^ b) for d in range(m)]) for b, part in enumerate(parts) if b
    ]

    ring = ring_of(4, across)
    spot = np.argsort(np.array(ring))
    routes = [[(ring[p], ring[(p + way) % n]) for p in range(n)] for way in (1, -1)]

    def owners(*offsets):
        return np.array([[ring[(spot[a] + o) % n] for o in offsets] for a in range(n)], np.int32)

    own = [jnp.stack(parts[:half]), jnp.stack(parts[half:])]
    tips = [[piece, piece] for piece in own]
    arrived, sums = [([own], [0])], None
    for s in range(1, n // 2 + 1):
        if s >= 3:
            ready = arrived[: s - 1] if s == 3 else arrived[s - 2 : s - 1]
            pieces, offsets = (sum(lists, []) for lists in zip(*ready))
            sums = project(pieces, owners(*offsets), sums, here, weights)
            tips[0], sums = lax.optimization_barrier((tips[0], sums))
        for h in range(2):
            for way in range(2) if s < n // 2 else [h]:
                tips[h][way] = lax.ppermute(tips[h][way], "ctx", routes[way])
        if s < n // 2:
            arrived.append(([list(piece) for piece in zip(*tips)], [-s, s]))
    pieces, offsets = arrived[-1]
    sums = project(pieces, owners(*offsets), sums, here, weights, grant=51)
    final = [[tips[0][0], tips[1][1]]]
    sent = project(final, owners(n // 2), sums, here, weights, last=True, grant=51)

    found = []
    for e in range(2):
        route = []
        for a in range(n):
            for b in range(m):
                route.append((a * m + b, row_block((a + e) % 2, b) * m + a // 2))
        found.append(lax.ppermute(sent[e], ("ctx", "ch"), route))
    even = (j // across) % 2 == 0
    return jnp.where(even, jnp.concatenate(found, axis=1), jnp.concatenate(found[::-1], axis=1))


def solution(mesh):
    placed = (
        P("ctx", "ch"),
        P("ctx", "ch"),
        P("ctx", "ch"),
        P("ctx", "ch"),
        P("ch"),
        P("ch", "ctx"),
    )
    return jax.shard_map(
        per_device, mesh=mesh, in_specs=placed, out_specs=P("ctx", "ch"), check_vma=False
    )
```

```python
import math

import jax
import jax.numpy as jnp
import numpy as np
from jax import lax
from jax.experimental import pallas as pl
from jax.experimental.pallas import tpu as pltpu
from jax.sharding import PartitionSpec as P

BF16, F32 = jnp.bfloat16, jnp.float32
MIB = 2**20


def tables(block):
    freqs = np.arange(block, dtype=np.float64)[:, None] + 0.5
    window = np.arange(-block, block, dtype=np.float64)[None, :]
    angles = math.pi / block * freqs * window
    forward = np.concatenate([np.cos(angles), -np.sin(angles)], axis=0)
    places = angles[:, block:].T
    inverse = np.concatenate([np.cos(places), -np.sin(places)], axis=1) / block
    return forward.astype(BF16), inverse.astype(BF16)


def pack_kernel(outer_ref, inner_ref, values_ref, filters_ref, out_ref):
    n, _, _, chans = out_ref.shape
    gated = (inner_ref[...].astype(F32) * values_ref[...].astype(F32)).astype(BF16)
    lags = filters_ref[...].astype(BF16)
    outer = outer_ref[...]
    for d in range(n):
        part = slice(d * chans, (d + 1) * chans)
        out_ref[d, 0] = gated[:, part]
        out_ref[d, 1] = lags[:, part]
        out_ref[d, 2] = outer[:, part]


def pack(outer_gate, inner_gate, values_in, filters, n):
    block, wide = outer_gate.shape
    tile = block // 2
    return pl.pallas_call(
        pack_kernel,
        grid=(block // tile,),
        in_specs=[pl.BlockSpec((tile, wide), lambda t: (t, 0))] * 4,
        out_specs=pl.BlockSpec((n, 3, tile, wide // n), lambda t: (0, 0, t, 0)),
        out_shape=jax.ShapeDtypeStruct((n, 3, block, wide // n), BF16),
        compiler_params=pltpu.CompilerParams(vmem_limit_bytes=60 * MIB),
        cost_estimate=pl.CostEstimate(flops=2**18, bytes_accessed=4 * MIB, transcendentals=0),
        name="pack",
    )(outer_gate, inner_gate, values_in, filters)


def conv_kernel(places, here_ref, in_ref, skip_ref, fwd_ref, inv_ref, *rest):
    mixes, (xs, gs, ys, mix_ref) = rest[:-4], rest[-4:]
    n, _, block, chans = in_ref.shape
    empty = jnp.zeros((block, chans), BF16)
    for k in range(0, n, 2):
        pair = jnp.concatenate([in_ref[k, 0], in_ref[k + 1, 0]], axis=1)
        both = jnp.dot(fwd_ref[:, block:], pair, preferred_element_type=F32)
        xs[k], xs[k + 1] = both[:, :chans], both[:, chans:]
        pair = jnp.concatenate([in_ref[k, 1], in_ref[k + 1, 1]], axis=1)
        both = jnp.dot(fwd_ref[:, block:], pair, preferred_element_type=F32)
        pair = jnp.concatenate([in_ref[k - 1, 1] if k else empty, in_ref[k, 1]], axis=1)
        both += jnp.dot(fwd_ref[:, :block], pair, preferred_element_type=F32)
        gs[k], gs[k + 1] = both[:, :chans], both[:, chans:]

    step = 8

    @pl.loop(0, block // step)
    def _(c):
        re = pl.ds(pl.multiple_of(c * step, step), step)
        im = pl.ds(pl.multiple_of(block + c * step, step), step)
        xr = [xs[k, re, :] for k in range(n)]
        xi = [xs[k, im, :] for k in range(n)]
        gr = [gs[k, re, :] for k in range(n)]
        gi = [gs[k, im, :] for k in range(n)]
        xt = [a + b for a, b in zip(xr, xi)]
        gt = [a + b for a, b in zip(gr, gi)]
        for i in range(n):
            one = xr[0] * gr[i]
            two = xi[0] * gi[i]
            three = xt[0] * gt[i]
            for k in range(1, i + 1):
                one += xr[k] * gr[i - k]
                two += xi[k] * gi[i - k]
                three += xt[k] * gt[i - k]
            ys[i, re, :] = one - two
            ys[i, im, :] = three - (one + two)

    for k in range(0, n, 2):
        pair = jnp.concatenate([ys[k].astype(BF16), ys[k + 1].astype(BF16)], axis=1)
        both = jnp.dot(inv_ref[...], pair, preferred_element_type=F32)
        for i, conv in ((k, both[:, :chans]), (k + 1, both[:, chans:])):
            mix = in_ref[i, 2].astype(F32) * (conv + skip_ref[...] * in_ref[i, 0].astype(F32))
            chunk, place = places[i]
            mix_ref[place, chunk] = mix.astype(BF16)
    for b, ref in enumerate(mixes):
        ref[...] = mix_ref[lax.bitwise_xor(here_ref[1], b)]


def convolve(here, packed, skip, places):
    n, _, block, chans = packed.shape
    m = n // 2
    forward, inverse = tables(block)

    held = pl.BlockSpec(memory_space=pltpu.VMEM)
    return pl.pallas_call(
        lambda *refs: conv_kernel(places, *refs),
        grid_spec=pltpu.PrefetchScalarGridSpec(
            num_scalar_prefetch=1,
            grid=(1,),
            in_specs=[held] * 4,
            out_specs=[held] * m,
            scratch_shapes=[pltpu.VMEM((n, 2 * block, chans), F32)] * 3
            + [pltpu.VMEM((m, 2, block, chans), BF16)],
        ),
        out_shape=[jax.ShapeDtypeStruct((2, block, chans), BF16)] * m,
        compiler_params=pltpu.CompilerParams(vmem_limit_bytes=20 * MIB),
        cost_estimate=pl.CostEstimate(flops=2**31, bytes_accessed=4 * MIB, transcendentals=0),
        name="convolve",
    )(here, packed, skip, jnp.asarray(forward), jnp.asarray(inverse))


def project_kernel(count, m, last, here_ref, table_ref, *refs):
    refs = list(refs)
    total = refs.pop(0)[...] if len(refs) > (2 + m) * count + 1 + last else None
    for _ in range(count):
        piece, slabs = refs[:2], refs[2 : 2 + m]
        del refs[: 2 + m]
        share = m // 2
        left = [piece[b // share][b % share] for b in range(m)]
        term = jnp.dot(
            jnp.concatenate([a.reshape(-1, a.shape[-1]) for a in left], axis=1),
            jnp.concatenate([slab[0] for slab in slabs], axis=0),
            preferred_element_type=F32,
        )
        total = term if total is None else total + term
    if last:
        total = total.astype(BF16)
        block = total.shape[0] // 2
        chunks = [total[:block], total[block:]]

        @pl.when(lax.rem(here_ref[0], 2) == 0)
        def _():
            refs[0][...], refs[1][...] = chunks

        @pl.when(lax.rem(here_ref[0], 2) == 1)
        def _():
            refs[1][...], refs[0][...] = chunks
    else:
        refs[0][...] = total


def project(pieces, owners, total, here, weights, last=False, grant=60):
    m, count = len(weights), len(pieces)
    _, chans, columns = weights[0].shape
    block = pieces[0][0].shape[-2]
    operands, specs = [], []

    def whole(shape):
        if last:
            return pl.BlockSpec(memory_space=pltpu.VMEM)
        return pl.BlockSpec(shape, lambda t, *_: (0,) * len(shape))

    if total is not None:
        operands.append(total)
        specs.append(whole(total.shape))
    for s, piece in enumerate(pieces):
        operands += list(piece) + weights
        specs += [whole(part.shape) for part in piece]

        def rows(t, here, table, s=s):
            return (table[here[0] * count + s], 0, 0)

        specs += [pl.BlockSpec((1, chans, columns), rows)] * m
    outs = [((block, columns), BF16)] * 2 if last else [((2 * block, columns), F32)]
    found = pl.pallas_call(
        lambda *refs: project_kernel(count, m, last, *refs),
        grid_spec=pltpu.PrefetchScalarGridSpec(
            num_scalar_prefetch=2,
            grid=(1,),
            in_specs=specs,
            out_specs=[whole(size) for size, _ in outs],
        ),
        out_shape=[jax.ShapeDtypeStruct(*out) for out in outs],
        compiler_params=pltpu.CompilerParams(vmem_limit_bytes=grant * MIB),
        cost_estimate=pl.CostEstimate(flops=0, bytes_accessed=0, transcendentals=0),
        name="project",
    )(here, jnp.asarray(owners.reshape(-1)), *operands)
    return found if last else found[0]


def ring_of(deep, across):
    walk = []
    for a in range(across):
        column = list(range(1, deep))
        walk += [d * across + a for d in (column if a % 2 == 0 else column[::-1])]
    return walk + [a for a in reversed(range(across))]


def per_device(outer_gate, inner_gate, values_in, filters, skip_gain, w_out):
    n, m = lax.axis_size("ctx"), lax.axis_size("ch")
    j, k = lax.axis_index("ctx"), lax.axis_index("ch")
    block, wide = outer_gate.shape
    chans = wide // n
    across = n // 4
    half = m // 2
    assert n == 2 * m
    here = jnp.stack([j, k]).astype(jnp.int32)

    def row_block(h, d):
        return (h + 2 * (d % 2)) * across + d // 2

    places = {row_block(h, d): (h, d) for h in range(2) for d in range(m)}

    weights = [w_out.reshape(n, chans, -1)]
    while len(weights) < m:
        pairs = [(d, d ^ len(weights)) for d in range(m)]
        if len(weights) == 1:
            weights.append(lax.ppermute(weights[0], "ch", pairs))
        else:
            for even in list(weights[::2]):
                far = lax.ppermute(even, "ch", pairs)
                weights += [far, lax.ppermute(far, "ch", [(d, d ^ 1) for d in range(m)])]

    packed = pack(outer_gate, inner_gate, values_in, filters, n)
    packed = lax.all_to_all(packed, "ctx", 0, 0)
    skip = lax.dynamic_slice_in_dim(skip_gain, j * chans, chans, 0)[None, :]
    packed, weights = lax.optimization_barrier((packed, weights))
    parts = list(convolve(here, packed, skip, places))
    parts = parts[:1] + [
        lax.ppermute(part, "ch", [(d, d ^ b) for d in range(m)]) for b, part in enumerate(parts) if b
    ]

    ring = ring_of(4, across)
    spot = np.argsort(np.array(ring))
    routes = [[(ring[p], ring[(p + way) % n]) for p in range(n)] for way in (1, -1)]

    def owners(*offsets):
        return np.array([[ring[(spot[a] + o) % n] for o in offsets] for a in range(n)], np.int32)

    own = [jnp.stack(parts[:half]), jnp.stack(parts[half:])]
    tips = [[piece, piece] for piece in own]
    arrived, sums = [([own], [0])], None
    for s in range(1, n // 2 + 1):
        if s >= 3:
            ready = arrived[: s - 1] if s == 3 else arrived[s - 2 : s - 1]
            pieces, offsets = (sum(lists, []) for lists in zip(*ready))
            sums = project(pieces, owners(*offsets), sums, here, weights)
            tips[0], sums = lax.optimization_barrier((tips[0], sums))
        for h in range(2):
            for way in range(2) if s < n // 2 else [h]:
                tips[h][way] = lax.ppermute(tips[h][way], "ctx", routes[way])
        if s < n // 2:
            arrived.append(([list(piece) for piece in zip(*tips)], [-s, s]))
    pieces, offsets = arrived[-1]
    sums = project(pieces, owners(*offsets), sums, here, weights, grant=51)
    final = [[tips[0][0], tips[1][1]]]
    sent = project(final, owners(n // 2), sums, here, weights, last=True, grant=51)

    found = []
    for e in range(2):
        route = []
        for a in range(n):
            for b in range(m):
                route.append((a * m + b, row_block((a + e) % 2, b) * m + a // 2))
        found.append(lax.ppermute(sent[e], ("ctx", "ch"), route))
    even = (j // across) % 2 == 0
    return jnp.where(even, jnp.concatenate(found, axis=1), jnp.concatenate(found[::-1], axis=1))


def solution(mesh):
    placed = (
        P("ctx", "ch"),
        P("ctx", "ch"),
        P("ctx", "ch"),
        P("ctx", "ch"),
        P("ch"),
        P("ch", "ctx"),
    )
    return jax.shard_map(
        per_device, mesh=mesh, in_specs=placed, out_specs=P("ctx", "ch"), check_vma=False
    )
```

```python
import math

import jax
import jax.numpy as jnp
import numpy as np
from jax import lax
from jax.experimental import pallas as pl
from jax.experimental.pallas import tpu as pltpu
from jax.sharding import PartitionSpec as P

BF16, F32 = jnp.bfloat16, jnp.float32
MIB = 2**20


def tables(block):
    freqs = np.arange(block, dtype=np.float64)[:, None] + 0.5
    window = np.arange(-block, block, dtype=np.float64)[None, :]
    angles = math.pi / block * freqs * window
    forward = np.concatenate([np.cos(angles), -np.sin(angles)], axis=0)
    places = angles[:, block:].T
    inverse = np.concatenate([np.cos(places), -np.sin(places)], axis=1) / block
    return forward.astype(BF16), inverse.astype(BF16)


def pack_kernel(outer_ref, inner_ref, values_ref, filters_ref, out_ref):
    n, _, _, chans = out_ref.shape
    gated = (inner_ref[...].astype(F32) * values_ref[...].astype(F32)).astype(BF16)
    lags = filters_ref[...].astype(BF16)
    outer = outer_ref[...]
    for d in range(n):
        part = slice(d * chans, (d + 1) * chans)
        out_ref[d, 0] = gated[:, part]
        out_ref[d, 1] = lags[:, part]
        out_ref[d, 2] = outer[:, part]


def pack(outer_gate, inner_gate, values_in, filters, n):
    block, wide = outer_gate.shape
    tile = block // 2
    return pl.pallas_call(
        pack_kernel,
        grid=(block // tile,),
        in_specs=[pl.BlockSpec((tile, wide), lambda t: (t, 0))] * 4,
        out_specs=pl.BlockSpec((n, 3, tile, wide // n), lambda t: (0, 0, t, 0)),
        out_shape=jax.ShapeDtypeStruct((n, 3, block, wide // n), BF16),
        compiler_params=pltpu.CompilerParams(vmem_limit_bytes=60 * MIB),
        cost_estimate=pl.CostEstimate(flops=2**18, bytes_accessed=4 * MIB, transcendentals=0),
        name="pack",
    )(outer_gate, inner_gate, values_in, filters)


def conv_kernel(places, here_ref, in_ref, skip_ref, fwd_ref, inv_ref, *rest):
    mixes, (xs, gs, ys, mix_ref) = rest[:-4], rest[-4:]
    n, _, block, chans = in_ref.shape
    empty = jnp.zeros((block, chans), BF16)
    for k in range(0, n, 2):
        pair = jnp.concatenate([in_ref[k, 0], in_ref[k + 1, 0]], axis=1)
        both = jnp.dot(fwd_ref[:, block:], pair, preferred_element_type=F32)
        xs[k], xs[k + 1] = both[:, :chans], both[:, chans:]
        pair = jnp.concatenate([in_ref[k, 1], in_ref[k + 1, 1]], axis=1)
        both = jnp.dot(fwd_ref[:, block:], pair, preferred_element_type=F32)
        pair = jnp.concatenate([in_ref[k - 1, 1] if k else empty, in_ref[k, 1]], axis=1)
        both += jnp.dot(fwd_ref[:, :block], pair, preferred_element_type=F32)
        gs[k], gs[k + 1] = both[:, :chans], both[:, chans:]

    step = 8

    @pl.loop(0, block // step)
    def _(c):
        re = pl.ds(pl.multiple_of(c * step, step), step)
        im = pl.ds(pl.multiple_of(block + c * step, step), step)
        xr = [xs[k, re, :] for k in range(n)]
        xi = [xs[k, im, :] for k in range(n)]
        gr = [gs[k, re, :] for k in range(n)]
        gi = [gs[k, im, :] for k in range(n)]
        xt = [a + b for a, b in zip(xr, xi)]
        gt = [a + b for a, b in zip(gr, gi)]
        for i in range(n):
            one = xr[0] * gr[i]
            two = xi[0] * gi[i]
            three = xt[0] * gt[i]
            for k in range(1, i + 1):
                one += xr[k] * gr[i - k]
                two += xi[k] * gi[i - k]
                three += xt[k] * gt[i - k]
            ys[i, re, :] = one - two
            ys[i, im, :] = three - (one + two)

    for k in range(0, n, 2):
        pair = jnp.concatenate([ys[k].astype(BF16), ys[k + 1].astype(BF16)], axis=1)
        both = jnp.dot(inv_ref[...], pair, preferred_element_type=F32)
        for i, conv in ((k, both[:, :chans]), (k + 1, both[:, chans:])):
            mix = in_ref[i, 2].astype(F32) * (conv + skip_ref[...] * in_ref[i, 0].astype(F32))
            chunk, place = places[i]
            mix_ref[place, chunk] = mix.astype(BF16)
    for b, ref in enumerate(mixes):
        ref[...] = mix_ref[lax.bitwise_xor(here_ref[1], b)]


def convolve(here, packed, skip, places):
    n, _, block, chans = packed.shape
    m = n // 2
    forward, inverse = tables(block)

    held = pl.BlockSpec(memory_space=pltpu.VMEM)
    return pl.pallas_call(
        lambda *refs: conv_kernel(places, *refs),
        grid_spec=pltpu.PrefetchScalarGridSpec(
            num_scalar_prefetch=1,
            grid=(1,),
            in_specs=[held] * 4,
            out_specs=[held] * m,
            scratch_shapes=[pltpu.VMEM((n, 2 * block, chans), F32)] * 3
            + [pltpu.VMEM((m, 2, block, chans), BF16)],
        ),
        out_shape=[jax.ShapeDtypeStruct((2, block, chans), BF16)] * m,
        compiler_params=pltpu.CompilerParams(vmem_limit_bytes=20 * MIB),
        cost_estimate=pl.CostEstimate(flops=2**31, bytes_accessed=4 * MIB, transcendentals=0),
        name="convolve",
    )(here, packed, skip, jnp.asarray(forward), jnp.asarray(inverse))


def project_kernel(count, m, last, here_ref, table_ref, *refs):
    refs = list(refs)
    total = refs.pop(0)[...] if len(refs) > (2 + m) * count + 1 + last else None
    for _ in range(count):
        piece, slabs = refs[:2], refs[2 : 2 + m]
        del refs[: 2 + m]
        share = m // 2
        left = [piece[b // share][b % share] for b in range(m)]
        term = jnp.dot(
            jnp.concatenate([a.reshape(-1, a.shape[-1]) for a in left], axis=1),
            jnp.concatenate([slab[0] for slab in slabs], axis=0),
            preferred_element_type=F32,
        )
        total = term if total is None else total + term
    if last:
        total = total.astype(BF16)
        block = total.shape[0] // 2
        chunks = [total[:block], total[block:]]

        @pl.when(lax.rem(here_ref[0], 2) == 0)
        def _():
            refs[0][...], refs[1][...] = chunks

        @pl.when(lax.rem(here_ref[0], 2) == 1)
        def _():
            refs[1][...], refs[0][...] = chunks
    else:
        refs[0][...] = total


def project(pieces, owners, total, here, weights, last=False, grant=60):
    m, count = len(weights), len(pieces)
    _, chans, columns = weights[0].shape
    block = pieces[0][0].shape[-2]
    operands, specs = [], []

    def whole(shape):
        if last:
            return pl.BlockSpec(memory_space=pltpu.VMEM)
        return pl.BlockSpec(shape, lambda t, *_: (0,) * len(shape))

    if total is not None:
        operands.append(total)
        specs.append(whole(total.shape))
    for s, piece in enumerate(pieces):
        operands += list(piece) + weights
        specs += [whole(part.shape) for part in piece]

        def rows(t, here, table, s=s):
            return (table[here[0] * count + s], 0, 0)

        specs += [pl.BlockSpec((1, chans, columns), rows)] * m
    outs = [((block, columns), BF16)] * 2 if last else [((2 * block, columns), F32)]
    found = pl.pallas_call(
        lambda *refs: project_kernel(count, m, last, *refs),
        grid_spec=pltpu.PrefetchScalarGridSpec(
            num_scalar_prefetch=2,
            grid=(1,),
            in_specs=specs,
            out_specs=[whole(size) for size, _ in outs],
        ),
        out_shape=[jax.ShapeDtypeStruct(*out) for out in outs],
        compiler_params=pltpu.CompilerParams(vmem_limit_bytes=grant * MIB),
        cost_estimate=pl.CostEstimate(flops=0, bytes_accessed=0, transcendentals=0),
        name="project",
    )(here, jnp.asarray(owners.reshape(-1)), *operands)
    return found if last else found[0]


def ring_of(deep, across):
    walk = []
    for a in range(across):
        column = list(range(1, deep))
        walk += [d * across + a for d in (column if a % 2 == 0 else column[::-1])]
    return walk + [a for a in reversed(range(across))]


def per_device(outer_gate, inner_gate, values_in, filters, skip_gain, w_out):
    n, m = lax.axis_size("ctx"), lax.axis_size("ch")
    j, k = lax.axis_index("ctx"), lax.axis_index("ch")
    block, wide = outer_gate.shape
    chans = wide // n
    across = n // 4
    half = m // 2
    assert n == 2 * m
    here = jnp.stack([j, k]).astype(jnp.int32)

    def row_block(h, d):
        return 2 * (d % 2 * half + d // 2) + h

    places = {row_block(h, d): (h, d) for h in range(2) for d in range(m)}

    weights = [w_out.reshape(n, chans, -1)]
    while len(weights) < m:
        pairs = [(d, d ^ len(weights)) for d in range(m)]
        if len(weights) == 1:
            weights.append(lax.ppermute(weights[0], "ch", pairs))
        else:
            for even in list(weights[::2]):
                far = lax.ppermute(even, "ch", pairs)
                weights += [far, lax.ppermute(far, "ch", [(d, d ^ 1) for d in range(m)])]

    packed = pack(outer_gate, inner_gate, values_in, filters, n)
    packed = lax.all_to_all(packed, "ctx", 0, 0)
    skip = lax.dynamic_slice_in_dim(skip_gain, j * chans, chans, 0)[None, :]
    packed, weights = lax.optimization_barrier((packed, weights))
    parts = list(convolve(here, packed, skip, places))
    parts = parts[:1] + [
        lax.ppermute(part, "ch", [(d, d ^ b) for d in range(m)]) for b, part in enumerate(parts) if b
    ]

    ring = ring_of(4, across)
    spot = np.argsort(np.array(ring))
    routes = [[(ring[p], ring[(p + way) % n]) for p in range(n)] for way in (1, -1)]

    def owners(*offsets):
        return np.array([[ring[(spot[a] + o) % n] for o in offsets] for a in range(n)], np.int32)

    own = [jnp.stack(parts[:half]), jnp.stack(parts[half:])]
    tips = [[piece, piece] for piece in own]
    arrived, sums = [([own], [0])], None
    for s in range(1, n // 2 + 1):
        if s >= 3:
            ready = arrived[: s - 1] if s == 3 else arrived[s - 2 : s - 1]
            pieces, offsets = (sum(lists, []) for lists in zip(*ready))
            sums = project(pieces, owners(*offsets), sums, here, weights)
            tips[0], sums = lax.optimization_barrier((tips[0], sums))
        for h in range(2):
            for way in range(2) if s < n // 2 else [h]:
                tips[h][way] = lax.ppermute(tips[h][way], "ctx", routes[way])
        if s < n // 2:
            arrived.append(([list(piece) for piece in zip(*tips)], [-s, s]))
    pieces, offsets = arrived[-1]
    sums = project(pieces, owners(*offsets), sums, here, weights, grant=51)
    final = [[tips[0][0], tips[1][1]]]
    sent = project(final, owners(n // 2), sums, here, weights, last=True, grant=51)

    found = []
    for e in range(2):
        route = []
        for a in range(n):
            for b in range(m):
                route.append((a * m + b, row_block((a + e) % 2, b) * m + a // 2))
        found.append(lax.ppermute(sent[e], ("ctx", "ch"), route))
    even = j % 2 == 0
    return jnp.where(even, jnp.concatenate(found, axis=1), jnp.concatenate(found[::-1], axis=1))


def solution(mesh):
    placed = (
        P("ctx", "ch"),
        P("ctx", "ch"),
        P("ctx", "ch"),
        P("ctx", "ch"),
        P("ch"),
        P("ch", "ctx"),
    )
    return jax.shard_map(
        per_device, mesh=mesh, in_specs=placed, out_specs=P("ctx", "ch"), check_vma=False
    )
```

```python
import math

import jax
import jax.numpy as jnp
import numpy as np
from jax import lax
from jax.experimental import pallas as pl
from jax.experimental.pallas import tpu as pltpu
from jax.sharding import PartitionSpec as P

BF16, F32 = jnp.bfloat16, jnp.float32
MIB = 2**20


def tables(block):
    freqs = np.arange(block, dtype=np.float64)[:, None] + 0.5
    window = np.arange(-block, block, dtype=np.float64)[None, :]
    angles = math.pi / block * freqs * window
    forward = np.concatenate([np.cos(angles), -np.sin(angles)], axis=0)
    places = angles[:, block:].T
    inverse = np.concatenate([np.cos(places), -np.sin(places)], axis=1) / block
    return forward.astype(BF16), inverse.astype(BF16)


def pack_kernel(outer_ref, inner_ref, values_ref, filters_ref, out_ref):
    n, _, _, chans = out_ref.shape
    gated = (inner_ref[...].astype(F32) * values_ref[...].astype(F32)).astype(BF16)
    lags = filters_ref[...].astype(BF16)
    outer = outer_ref[...]
    for d in range(n):
        part = slice(d * chans, (d + 1) * chans)
        out_ref[d, 0] = gated[:, part]
        out_ref[d, 1] = lags[:, part]
        out_ref[d, 2] = outer[:, part]


def pack(outer_gate, inner_gate, values_in, filters, n):
    block, wide = outer_gate.shape
    tile = block
    return pl.pallas_call(
        pack_kernel,
        grid=(block // tile,),
        in_specs=[pl.BlockSpec((tile, wide), lambda t: (t, 0))] * 4,
        out_specs=pl.BlockSpec((n, 3, tile, wide // n), lambda t: (0, 0, t, 0)),
        out_shape=jax.ShapeDtypeStruct((n, 3, block, wide // n), BF16),
        compiler_params=pltpu.CompilerParams(vmem_limit_bytes=60 * MIB),
        cost_estimate=pl.CostEstimate(flops=2**18, bytes_accessed=4 * MIB, transcendentals=0),
        name="pack",
    )(outer_gate, inner_gate, values_in, filters)


def conv_kernel(places, here_ref, in_ref, skip_ref, fwd_ref, inv_ref, *rest):
    mixes, (xs, gs, ys, mix_ref) = rest[:-4], rest[-4:]
    n, _, block, chans = in_ref.shape
    empty = jnp.zeros((block, chans), BF16)
    for k in range(0, n, 2):
        pair = jnp.concatenate([in_ref[k, 0], in_ref[k + 1, 0]], axis=1)
        both = jnp.dot(fwd_ref[:, block:], pair, preferred_element_type=F32)
        xs[k], xs[k + 1] = both[:, :chans], both[:, chans:]
        pair = jnp.concatenate([in_ref[k, 1], in_ref[k + 1, 1]], axis=1)
        both = jnp.dot(fwd_ref[:, block:], pair, preferred_element_type=F32)
        pair = jnp.concatenate([in_ref[k - 1, 1] if k else empty, in_ref[k, 1]], axis=1)
        both += jnp.dot(fwd_ref[:, :block], pair, preferred_element_type=F32)
        gs[k], gs[k + 1] = both[:, :chans], both[:, chans:]

    step = 8

    @pl.loop(0, block // step, unroll=2)
    def _(c):
        re = pl.ds(pl.multiple_of(c * step, step), step)
        im = pl.ds(pl.multiple_of(block + c * step, step), step)
        xr = [xs[k, re, :] for k in range(n)]
        xi = [xs[k, im, :] for k in range(n)]
        gr = [gs[k, re, :] for k in range(n)]
        gi = [gs[k, im, :] for k in range(n)]
        xt = [a + b for a, b in zip(xr, xi)]
        gt = [a + b for a, b in zip(gr, gi)]
        for i in range(n):
            one = xr[0] * gr[i]
            two = xi[0] * gi[i]
            three = xt[0] * gt[i]
            for k in range(1, i + 1):
                one += xr[k] * gr[i - k]
                two += xi[k] * gi[i - k]
                three += xt[k] * gt[i - k]
            ys[i, re, :] = one - two
            ys[i, im, :] = three - (one + two)

    for k in range(0, n, 2):
        pair = jnp.concatenate([ys[k].astype(BF16), ys[k + 1].astype(BF16)], axis=1)
        both = jnp.dot(inv_ref[...], pair, preferred_element_type=F32)
        for i, conv in ((k, both[:, :chans]), (k + 1, both[:, chans:])):
            mix = in_ref[i, 2].astype(F32) * (conv + skip_ref[...] * in_ref[i, 0].astype(F32))
            chunk, place = places[i]
            mix_ref[place, chunk] = mix.astype(BF16)
    for b, ref in enumerate(mixes):
        ref[...] = mix_ref[lax.bitwise_xor(here_ref[1], b)]


def convolve(here, packed, skip, places):
    n, _, block, chans = packed.shape
    m = n // 2
    forward, inverse = tables(block)

    held = pl.BlockSpec(memory_space=pltpu.VMEM)
    return pl.pallas_call(
        lambda *refs: conv_kernel(places, *refs),
        grid_spec=pltpu.PrefetchScalarGridSpec(
            num_scalar_prefetch=1,
            grid=(1,),
            in_specs=[held] * 4,
            out_specs=[held] * m,
            scratch_shapes=[pltpu.VMEM((n, 2 * block, chans), F32)] * 3
            + [pltpu.VMEM((m, 2, block, chans), BF16)],
        ),
        out_shape=[jax.ShapeDtypeStruct((2, block, chans), BF16)] * m,
        compiler_params=pltpu.CompilerParams(vmem_limit_bytes=20 * MIB),
        cost_estimate=pl.CostEstimate(flops=2**31, bytes_accessed=4 * MIB, transcendentals=0),
        name="convolve",
    )(here, packed, skip, jnp.asarray(forward), jnp.asarray(inverse))


def project_kernel(count, m, last, here_ref, table_ref, *refs):
    refs = list(refs)
    total = refs.pop(0)[...] if len(refs) > (2 + m) * count + 1 + last else None
    for _ in range(count):
        piece, slabs = refs[:2], refs[2 : 2 + m]
        del refs[: 2 + m]
        share = m // 2
        left = [piece[b // share][b % share] for b in range(m)]
        term = jnp.dot(
            jnp.concatenate([a.reshape(-1, a.shape[-1]) for a in left], axis=1),
            jnp.concatenate([slab[0] for slab in slabs], axis=0),
            preferred_element_type=F32,
        )
        total = term if total is None else total + term
    if last:
        total = total.astype(BF16)
        block = total.shape[0] // 2
        chunks = [total[:block], total[block:]]

        @pl.when(lax.rem(here_ref[0], 2) == 0)
        def _():
            refs[0][...], refs[1][...] = chunks

        @pl.when(lax.rem(here_ref[0], 2) == 1)
        def _():
            refs[1][...], refs[0][...] = chunks
    else:
        refs[0][...] = total


def project(pieces, owners, total, here, weights, last=False, grant=60):
    m, count = len(weights), len(pieces)
    _, chans, columns = weights[0].shape
    block = pieces[0][0].shape[-2]
    operands, specs = [], []

    def whole(shape):
        if last:
            return pl.BlockSpec(memory_space=pltpu.VMEM)
        return pl.BlockSpec(shape, lambda t, *_: (0,) * len(shape))

    if total is not None:
        operands.append(total)
        specs.append(whole(total.shape))
    for s, piece in enumerate(pieces):
        operands += list(piece) + weights
        specs += [whole(part.shape) for part in piece]

        def rows(t, here, table, s=s):
            return (table[here[0] * count + s], 0, 0)

        specs += [pl.BlockSpec((1, chans, columns), rows)] * m
    outs = [((block, columns), BF16)] * 2 if last else [((2 * block, columns), F32)]
    found = pl.pallas_call(
        lambda *refs: project_kernel(count, m, last, *refs),
        grid_spec=pltpu.PrefetchScalarGridSpec(
            num_scalar_prefetch=2,
            grid=(1,),
            in_specs=specs,
            out_specs=[whole(size) for size, _ in outs],
        ),
        out_shape=[jax.ShapeDtypeStruct(*out) for out in outs],
        compiler_params=pltpu.CompilerParams(vmem_limit_bytes=grant * MIB),
        cost_estimate=pl.CostEstimate(flops=0, bytes_accessed=0, transcendentals=0),
        name="project",
    )(here, jnp.asarray(owners.reshape(-1)), *operands)
    return found if last else found[0]


def ring_of(deep, across):
    walk = []
    for a in range(across):
        column = list(range(1, deep))
        walk += [d * across + a for d in (column if a % 2 == 0 else column[::-1])]
    return walk + [a for a in reversed(range(across))]


def per_device(outer_gate, inner_gate, values_in, filters, skip_gain, w_out):
    n, m = lax.axis_size("ctx"), lax.axis_size("ch")
    j, k = lax.axis_index("ctx"), lax.axis_index("ch")
    block, wide = outer_gate.shape
    chans = wide // n
    across = n // 4
    half = m // 2
    assert n == 2 * m
    here = jnp.stack([j, k]).astype(jnp.int32)

    def row_block(h, d):
        return (h + 2 * (d % 2)) * across + d // 2

    places = {row_block(h, d): (h, d) for h in range(2) for d in range(m)}

    weights = [w_out.reshape(n, chans, -1)]
    while len(weights) < m:
        pairs = [(d, d ^ len(weights)) for d in range(m)]
        if len(weights) == 1:
            weights.append(lax.ppermute(weights[0], "ch", pairs))
        else:
            for even in list(weights[::2]):
                far = lax.ppermute(even, "ch", pairs)
                weights += [far, lax.ppermute(far, "ch", [(d, d ^ 1) for d in range(m)])]

    packed = pack(outer_gate, inner_gate, values_in, filters, n)
    packed = lax.all_to_all(packed, "ctx", 0, 0)
    skip = lax.dynamic_slice_in_dim(skip_gain, j * chans, chans, 0)[None, :]
    packed, weights = lax.optimization_barrier((packed, weights))
    parts = list(convolve(here, packed, skip, places))
    parts = parts[:1] + [
        lax.ppermute(part, "ch", [(d, d ^ b) for d in range(m)]) for b, part in enumerate(parts) if b
    ]

    ring = ring_of(4, across)
    spot = np.argsort(np.array(ring))
    routes = [[(ring[p], ring[(p + way) % n]) for p in range(n)] for way in (1, -1)]

    def owners(*offsets):
        return np.array([[ring[(spot[a] + o) % n] for o in offsets] for a in range(n)], np.int32)

    own = [jnp.stack(parts[:half]), jnp.stack(parts[half:])]
    tips = [[piece, piece] for piece in own]
    arrived, sums = [([own], [0])], None
    for s in range(1, n // 2 + 1):
        if s >= 3:
            ready = arrived[: s - 1] if s == 3 else arrived[s - 2 : s - 1]
            pieces, offsets = (sum(lists, []) for lists in zip(*ready))
            sums = project(pieces, owners(*offsets), sums, here, weights)
            tips[0], sums = lax.optimization_barrier((tips[0], sums))
        for h in range(2):
            for way in range(2) if s < n // 2 else [h]:
                tips[h][way] = lax.ppermute(tips[h][way], "ctx", routes[way])
        if s < n // 2:
            arrived.append(([list(piece) for piece in zip(*tips)], [-s, s]))
    pieces, offsets = arrived[-1]
    sums = project(pieces, owners(*offsets), sums, here, weights, grant=51)
    final = [[tips[0][0], tips[1][1]]]
    sent = project(final, owners(n // 2), sums, here, weights, last=True, grant=51)

    found = []
    for e in range(2):
        route = []
        for a in range(n):
            for b in range(m):
                route.append((a * m + b, row_block((a + e) % 2, b) * m + a // 2))
        found.append(lax.ppermute(sent[e], ("ctx", "ch"), route))
    even = (j // across) % 2 == 0
    return jnp.where(even, jnp.concatenate(found, axis=1), jnp.concatenate(found[::-1], axis=1))


def solution(mesh):
    placed = (
        P("ctx", "ch"),
        P("ctx", "ch"),
        P("ctx", "ch"),
        P("ctx", "ch"),
        P("ch"),
        P("ch", "ctx"),
    )
    return jax.shard_map(
        per_device, mesh=mesh, in_specs=placed, out_specs=P("ctx", "ch"), check_vma=False
    )
```

```python
import math

import jax
import jax.numpy as jnp
import numpy as np
from jax import lax
from jax.experimental import pallas as pl
from jax.experimental.pallas import tpu as pltpu
from jax.sharding import PartitionSpec as P

BF16, F32 = jnp.bfloat16, jnp.float32
MIB = 2**20


def tables(block):
    freqs = np.arange(block, dtype=np.float64)[:, None] + 0.5
    window = np.arange(-block, block, dtype=np.float64)[None, :]
    angles = math.pi / block * freqs * window
    forward = np.concatenate([np.cos(angles), -np.sin(angles)], axis=0)
    places = angles[:, block:].T
    inverse = np.concatenate([np.cos(places), -np.sin(places)], axis=1) / block
    return forward.astype(BF16), inverse.astype(BF16)


def pack_kernel(outer_ref, inner_ref, values_ref, filters_ref, out_ref):
    n, _, _, chans = out_ref.shape
    gated = (inner_ref[...].astype(F32) * values_ref[...].astype(F32)).astype(BF16)
    lags = filters_ref[...].astype(BF16)
    outer = outer_ref[...]
    for d in range(n):
        part = slice(d * chans, (d + 1) * chans)
        out_ref[d, 0] = gated[:, part]
        out_ref[d, 1] = lags[:, part]
        out_ref[d, 2] = outer[:, part]


def pack(outer_gate, inner_gate, values_in, filters, n):
    block, wide = outer_gate.shape
    tile = block // 2
    return pl.pallas_call(
        pack_kernel,
        grid=(block // tile,),
        in_specs=[pl.BlockSpec((tile, wide), lambda t: (t, 0))] * 4,
        out_specs=pl.BlockSpec((n, 3, tile, wide // n), lambda t: (0, 0, t, 0)),
        out_shape=jax.ShapeDtypeStruct((n, 3, block, wide // n), BF16),
        compiler_params=pltpu.CompilerParams(vmem_limit_bytes=60 * MIB),
        cost_estimate=pl.CostEstimate(flops=2**18, bytes_accessed=4 * MIB, transcendentals=0),
        name="pack",
    )(outer_gate, inner_gate, values_in, filters)


def conv_kernel(places, here_ref, in_ref, skip_ref, fwd_ref, inv_ref, *rest):
    mixes, (xs, gs, ys, mix_ref) = rest[:-4], rest[-4:]
    n, _, block, chans = in_ref.shape
    empty = jnp.zeros((block, chans), BF16)
    for k in range(0, n, 2):
        pair = jnp.concatenate([in_ref[k, 0], in_ref[k + 1, 0]], axis=1)
        both = jnp.dot(fwd_ref[:, block:], pair, preferred_element_type=F32)
        xs[k], xs[k + 1] = both[:, :chans], both[:, chans:]
        pair = jnp.concatenate([in_ref[k, 1], in_ref[k + 1, 1]], axis=1)
        both = jnp.dot(fwd_ref[:, block:], pair, preferred_element_type=F32)
        pair = jnp.concatenate([in_ref[k - 1, 1] if k else empty, in_ref[k, 1]], axis=1)
        both += jnp.dot(fwd_ref[:, :block], pair, preferred_element_type=F32)
        gs[k], gs[k + 1] = both[:, :chans], both[:, chans:]

    step = 8

    @pl.loop(0, block // step, unroll=4)
    def _(c):
        re = pl.ds(pl.multiple_of(c * step, step), step)
        im = pl.ds(pl.multiple_of(block + c * step, step), step)
        xr = [xs[k, re, :] for k in range(n)]
        xi = [xs[k, im, :] for k in range(n)]
        gr = [gs[k, re, :] for k in range(n)]
        gi = [gs[k, im, :] for k in range(n)]
        xt = [a + b for a, b in zip(xr, xi)]
        gt = [a + b for a, b in zip(gr, gi)]
        for i in range(n):
            one = xr[0] * gr[i]
            two = xi[0] * gi[i]
            three = xt[0] * gt[i]
            for k in range(1, i + 1):
                one += xr[k] * gr[i - k]
                two += xi[k] * gi[i - k]
                three += xt[k] * gt[i - k]
            ys[i, re, :] = one - two
            ys[i, im, :] = three - (one + two)

    for k in range(0, n, 2):
        pair = jnp.concatenate([ys[k].astype(BF16), ys[k + 1].astype(BF16)], axis=1)
        both = jnp.dot(inv_ref[...], pair, preferred_element_type=F32)
        for i, conv in ((k, both[:, :chans]), (k + 1, both[:, chans:])):
            mix = in_ref[i, 2].astype(F32) * (conv + skip_ref[...] * in_ref[i, 0].astype(F32))
            chunk, place = places[i]
            mix_ref[place, chunk] = mix.astype(BF16)
    for b, ref in enumerate(mixes):
        ref[...] = mix_ref[lax.bitwise_xor(here_ref[1], b)]


def convolve(here, packed, skip, places):
    n, _, block, chans = packed.shape
    m = n // 2
    forward, inverse = tables(block)

    held = pl.BlockSpec(memory_space=pltpu.VMEM)
    return pl.pallas_call(
        lambda *refs: conv_kernel(places, *refs),
        grid_spec=pltpu.PrefetchScalarGridSpec(
            num_scalar_prefetch=1,
            grid=(1,),
            in_specs=[held] * 4,
            out_specs=[held] * m,
            scratch_shapes=[pltpu.VMEM((n, 2 * block, chans), F32)] * 3
            + [pltpu.VMEM((m, 2, block, chans), BF16)],
        ),
        out_shape=[jax.ShapeDtypeStruct((2, block, chans), BF16)] * m,
        compiler_params=pltpu.CompilerParams(vmem_limit_bytes=20 * MIB),
        cost_estimate=pl.CostEstimate(flops=2**31, bytes_accessed=4 * MIB, transcendentals=0),
        name="convolve",
    )(here, packed, skip, jnp.asarray(forward), jnp.asarray(inverse))


def project_kernel(count, m, last, here_ref, table_ref, *refs):
    refs = list(refs)
    total = refs.pop(0)[...] if len(refs) > (2 + m) * count + 1 + last else None
    for _ in range(count):
        piece, slabs = refs[:2], refs[2 : 2 + m]
        del refs[: 2 + m]
        share = m // 2
        left = [piece[b // share][b % share] for b in range(m)]
        term = jnp.dot(
            jnp.concatenate([a.reshape(-1, a.shape[-1]) for a in left], axis=1),
            jnp.concatenate([slab[0] for slab in slabs], axis=0),
            preferred_element_type=F32,
        )
        total = term if total is None else total + term
    if last:
        total = total.astype(BF16)
        block = total.shape[0] // 2
        chunks = [total[:block], total[block:]]

        @pl.when(lax.rem(here_ref[0], 2) == 0)
        def _():
            refs[0][...], refs[1][...] = chunks

        @pl.when(lax.rem(here_ref[0], 2) == 1)
        def _():
            refs[1][...], refs[0][...] = chunks
    else:
        refs[0][...] = total


def project(pieces, owners, total, here, weights, last=False, grant=60):
    m, count = len(weights), len(pieces)
    _, chans, columns = weights[0].shape
    block = pieces[0][0].shape[-2]
    operands, specs = [], []

    def whole(shape):
        if last:
            return pl.BlockSpec(memory_space=pltpu.VMEM)
        return pl.BlockSpec(shape, lambda t, *_: (0,) * len(shape))

    if total is not None:
        operands.append(total)
        specs.append(whole(total.shape))
    for s, piece in enumerate(pieces):
        operands += list(piece) + weights
        specs += [whole(part.shape) for part in piece]

        def rows(t, here, table, s=s):
            return (table[here[0] * count + s], 0, 0)

        specs += [pl.BlockSpec((1, chans, columns), rows)] * m
    outs = [((block, columns), BF16)] * 2 if last else [((2 * block, columns), F32)]
    found = pl.pallas_call(
        lambda *refs: project_kernel(count, m, last, *refs),
        grid_spec=pltpu.PrefetchScalarGridSpec(
            num_scalar_prefetch=2,
            grid=(1,),
            in_specs=specs,
            out_specs=[whole(size) for size, _ in outs],
        ),
        out_shape=[jax.ShapeDtypeStruct(*out) for out in outs],
        compiler_params=pltpu.CompilerParams(vmem_limit_bytes=grant * MIB),
        cost_estimate=pl.CostEstimate(flops=0, bytes_accessed=0, transcendentals=0),
        name="project",
    )(here, jnp.asarray(owners.reshape(-1)), *operands)
    return found if last else found[0]


def ring_of(deep, across):
    walk = []
    for a in range(across):
        column = list(range(1, deep))
        walk += [d * across + a for d in (column if a % 2 == 0 else column[::-1])]
    return walk + [a for a in reversed(range(across))]


def per_device(outer_gate, inner_gate, values_in, filters, skip_gain, w_out):
    n, m = lax.axis_size("ctx"), lax.axis_size("ch")
    j, k = lax.axis_index("ctx"), lax.axis_index("ch")
    block, wide = outer_gate.shape
    chans = wide // n
    across = n // 4
    half = m // 2
    assert n == 2 * m
    here = jnp.stack([j, k]).astype(jnp.int32)

    def row_block(h, d):
        return (h + 2 * (d % 2)) * across + d // 2

    places = {row_block(h, d): (h, d) for h in range(2) for d in range(m)}

    weights = [w_out.reshape(n, chans, -1)]
    while len(weights) < m:
        pairs = [(d, d ^ len(weights)) for d in range(m)]
        if len(weights) == 1:
            weights.append(lax.ppermute(weights[0], "ch", pairs))
        else:
            for even in list(weights[::2]):
                far = lax.ppermute(even, "ch", pairs)
                weights += [far, lax.ppermute(far, "ch", [(d, d ^ 1) for d in range(m)])]

    packed = pack(outer_gate, inner_gate, values_in, filters, n)
    packed = lax.all_to_all(packed, "ctx", 0, 0)
    skip = lax.dynamic_slice_in_dim(skip_gain, j * chans, chans, 0)[None, :]
    packed, weights = lax.optimization_barrier((packed, weights))
    parts = list(convolve(here, packed, skip, places))
    parts = parts[:1] + [
        lax.ppermute(part, "ch", [(d, d ^ b) for d in range(m)]) for b, part in enumerate(parts) if b
    ]

    ring = ring_of(4, across)
    spot = np.argsort(np.array(ring))
    routes = [[(ring[p], ring[(p + way) % n]) for p in range(n)] for way in (1, -1)]

    def owners(*offsets):
        return np.array([[ring[(spot[a] + o) % n] for o in offsets] for a in range(n)], np.int32)

    own = [jnp.stack(parts[:half]), jnp.stack(parts[half:])]
    tips = [[piece, piece] for piece in own]
    arrived, sums = [([own], [0])], None
    for s in range(1, n // 2 + 1):
        if s >= 3:
            ready = arrived[: s - 1] if s == 3 else arrived[s - 2 : s - 1]
            pieces, offsets = (sum(lists, []) for lists in zip(*ready))
            sums = project(pieces, owners(*offsets), sums, here, weights)
            tips[0], sums = lax.optimization_barrier((tips[0], sums))
        for h in range(2):
            for way in range(2) if s < n // 2 else [h]:
                tips[h][way] = lax.ppermute(tips[h][way], "ctx", routes[way])
        if s < n // 2:
            arrived.append(([list(piece) for piece in zip(*tips)], [-s, s]))
    pieces, offsets = arrived[-1]
    sums = project(pieces, owners(*offsets), sums, here, weights, grant=51)
    final = [[tips[0][0], tips[1][1]]]
    sent = project(final, owners(n // 2), sums, here, weights, last=True, grant=51)

    found = []
    for e in range(2):
        route = []
        for a in range(n):
            for b in range(m):
                route.append((a * m + b, row_block((a + e) % 2, b) * m + a // 2))
        found.append(lax.ppermute(sent[e], ("ctx", "ch"), route))
    even = (j // across) % 2 == 0
    return jnp.where(even, jnp.concatenate(found, axis=1), jnp.concatenate(found[::-1], axis=1))


def solution(mesh):
    placed = (
        P("ctx", "ch"),
        P("ctx", "ch"),
        P("ctx", "ch"),
        P("ctx", "ch"),
        P("ch"),
        P("ch", "ctx"),
    )
    return jax.shard_map(
        per_device, mesh=mesh, in_specs=placed, out_specs=P("ctx", "ch"), check_vma=False
    )
```

```python
import math

import jax
import jax.numpy as jnp
import numpy as np
from jax import lax
from jax.experimental import pallas as pl
from jax.experimental.pallas import tpu as pltpu
from jax.sharding import PartitionSpec as P

BF16, F32 = jnp.bfloat16, jnp.float32
MIB = 2**20


def tables(block):
    freqs = np.arange(block, dtype=np.float64)[:, None] + 0.5
    window = np.arange(-block, block, dtype=np.float64)[None, :]
    angles = math.pi / block * freqs * window
    forward = np.concatenate([np.cos(angles), -np.sin(angles)], axis=0)
    places = angles[:, block:].T
    inverse = np.concatenate([np.cos(places), -np.sin(places)], axis=1) / block
    return forward.astype(BF16), inverse.astype(BF16)


def pack_kernel(outer_ref, inner_ref, values_ref, filters_ref, out_ref):
    n, _, _, chans = out_ref.shape
    gated = (inner_ref[...].astype(F32) * values_ref[...].astype(F32)).astype(BF16)
    lags = filters_ref[...].astype(BF16)
    outer = outer_ref[...]
    for d in range(n):
        part = slice(d * chans, (d + 1) * chans)
        out_ref[d, 0] = gated[:, part]
        out_ref[d, 1] = lags[:, part]
        out_ref[d, 2] = outer[:, part]


def pack(outer_gate, inner_gate, values_in, filters, n):
    block, wide = outer_gate.shape
    tile = block // 2
    return pl.pallas_call(
        pack_kernel,
        grid=(block // tile,),
        in_specs=[pl.BlockSpec((tile, wide), lambda t: (t, 0))] * 4,
        out_specs=pl.BlockSpec((n, 3, tile, wide // n), lambda t: (0, 0, t, 0)),
        out_shape=jax.ShapeDtypeStruct((n, 3, block, wide // n), BF16),
        compiler_params=pltpu.CompilerParams(vmem_limit_bytes=60 * MIB),
        cost_estimate=pl.CostEstimate(flops=2**18, bytes_accessed=4 * MIB, transcendentals=0),
        name="pack",
    )(outer_gate, inner_gate, values_in, filters)


def conv_kernel(places, here_ref, in_ref, skip_ref, fwd_ref, inv_ref, *rest):
    mixes, (xs, gs, ys, mix_ref) = rest[:-4], rest[-4:]
    n, _, block, chans = in_ref.shape
    empty = jnp.zeros((block, chans), BF16)
    for k in range(0, n, 2):
        pair = jnp.concatenate([in_ref[k, 0], in_ref[k + 1, 0]], axis=1)
        both = jnp.dot(fwd_ref[:, block:], pair, preferred_element_type=F32)
        xs[k], xs[k + 1] = both[:, :chans], both[:, chans:]
        pair = jnp.concatenate([in_ref[k, 1], in_ref[k + 1, 1]], axis=1)
        both = jnp.dot(fwd_ref[:, block:], pair, preferred_element_type=F32)
        pair = jnp.concatenate([in_ref[k - 1, 1] if k else empty, in_ref[k, 1]], axis=1)
        both += jnp.dot(fwd_ref[:, :block], pair, preferred_element_type=F32)
        gs[k], gs[k + 1] = both[:, :chans], both[:, chans:]

    step = 8

    @pl.loop(0, block // step)
    def _(c):
        re = pl.ds(pl.multiple_of(c * step, step), step)
        im = pl.ds(pl.multiple_of(block + c * step, step), step)
        xr = [xs[k, re, :] for k in range(n)]
        xi = [xs[k, im, :] for k in range(n)]
        gr = [gs[k, re, :] for k in range(n)]
        gi = [gs[k, im, :] for k in range(n)]
        xt = [a + b for a, b in zip(xr, xi)]
        gt = [a + b for a, b in zip(gr, gi)]
        for i in range(n):
            one = xr[0] * gr[i]
            two = xi[0] * gi[i]
            three = xt[0] * gt[i]
            for k in range(1, i + 1):
                one += xr[k] * gr[i - k]
                two += xi[k] * gi[i - k]
                three += xt[k] * gt[i - k]
            ys[i, re, :] = one - two
            ys[i, im, :] = three - (one + two)

    for k in range(0, n, 2):
        pair = jnp.concatenate([ys[k].astype(BF16), ys[k + 1].astype(BF16)], axis=1)
        both = jnp.dot(inv_ref[...], pair, preferred_element_type=F32)
        for i, conv in ((k, both[:, :chans]), (k + 1, both[:, chans:])):
            mix = in_ref[i, 2].astype(F32) * (conv + skip_ref[...] * in_ref[i, 0].astype(F32))
            chunk, place = places[i]
            mix_ref[place, chunk] = mix.astype(BF16)
    for b, ref in enumerate(mixes):
        ref[...] = mix_ref[lax.bitwise_xor(here_ref[1], b)]


def convolve(here, packed, skip, places):
    n, _, block, chans = packed.shape
    m = n // 2
    forward, inverse = tables(block)

    held = pl.BlockSpec(memory_space=pltpu.VMEM)
    return pl.pallas_call(
        lambda *refs: conv_kernel(places, *refs),
        grid_spec=pltpu.PrefetchScalarGridSpec(
            num_scalar_prefetch=1,
            grid=(1,),
            in_specs=[held] * 4,
            out_specs=[held] * m,
            scratch_shapes=[pltpu.VMEM((n, 2 * block, chans), F32)] * 3
            + [pltpu.VMEM((m, 2, block, chans), BF16)],
        ),
        out_shape=[jax.ShapeDtypeStruct((2, block, chans), BF16)] * m,
        compiler_params=pltpu.CompilerParams(vmem_limit_bytes=20 * MIB),
        cost_estimate=pl.CostEstimate(flops=2**31, bytes_accessed=4 * MIB, transcendentals=0),
        name="convolve",
    )(here, packed, skip, jnp.asarray(forward), jnp.asarray(inverse))


def project_kernel(count, m, last, here_ref, table_ref, *refs):
    refs = list(refs)
    total = refs.pop(0)[...] if len(refs) > (2 + m) * count + 1 + last else None
    for _ in range(count):
        piece, slabs = refs[:2], refs[2 : 2 + m]
        del refs[: 2 + m]
        share = m // 2
        left = [piece[b // share][b % share] for b in range(m)]
        term = jnp.dot(
            jnp.concatenate([a.reshape(-1, a.shape[-1]) for a in left], axis=1),
            jnp.concatenate([slab[0] for slab in slabs], axis=0),
            preferred_element_type=F32,
        )
        total = term if total is None else total + term
    if last:
        total = total.astype(BF16)
        block = total.shape[0] // 2
        chunks = [total[:block], total[block:]]

        @pl.when(lax.rem(here_ref[0], 2) == 0)
        def _():
            refs[0][...], refs[1][...] = chunks

        @pl.when(lax.rem(here_ref[0], 2) == 1)
        def _():
            refs[1][...], refs[0][...] = chunks
    else:
        refs[0][...] = total


def project(pieces, owners, total, here, weights, last=False, grant=51):
    m, count = len(weights), len(pieces)
    _, chans, columns = weights[0].shape
    block = pieces[0][0].shape[-2]
    operands, specs = [], []

    def whole(shape):
        if last:
            return pl.BlockSpec(memory_space=pltpu.VMEM)
        return pl.BlockSpec(shape, lambda t, *_: (0,) * len(shape))

    if total is not None:
        operands.append(total)
        specs.append(whole(total.shape))
    for s, piece in enumerate(pieces):
        operands += list(piece) + weights
        specs += [whole(part.shape) for part in piece]

        def rows(t, here, table, s=s):
            return (table[here[0] * count + s], 0, 0)

        specs += [pl.BlockSpec((1, chans, columns), rows)] * m
    outs = [((block, columns), BF16)] * 2 if last else [((2 * block, columns), F32)]
    found = pl.pallas_call(
        lambda *refs: project_kernel(count, m, last, *refs),
        grid_spec=pltpu.PrefetchScalarGridSpec(
            num_scalar_prefetch=2,
            grid=(1,),
            in_specs=specs,
            out_specs=[whole(size) for size, _ in outs],
        ),
        out_shape=[jax.ShapeDtypeStruct(*out) for out in outs],
        compiler_params=pltpu.CompilerParams(vmem_limit_bytes=grant * MIB),
        cost_estimate=pl.CostEstimate(flops=0, bytes_accessed=0, transcendentals=0),
        name="project",
    )(here, jnp.asarray(owners.reshape(-1)), *operands)
    return found if last else found[0]


def ring_of(deep, across):
    walk = []
    for a in range(across):
        column = list(range(1, deep))
        walk += [d * across + a for d in (column if a % 2 == 0 else column[::-1])]
    return walk + [a for a in reversed(range(across))]


def per_device(outer_gate, inner_gate, values_in, filters, skip_gain, w_out):
    n, m = lax.axis_size("ctx"), lax.axis_size("ch")
    j, k = lax.axis_index("ctx"), lax.axis_index("ch")
    block, wide = outer_gate.shape
    chans = wide // n
    across = n // 4
    half = m // 2
    assert n == 2 * m
    here = jnp.stack([j, k]).astype(jnp.int32)

    def row_block(h, d):
        return (h + 2 * (d % 2)) * across + d // 2

    places = {row_block(h, d): (h, d) for h in range(2) for d in range(m)}

    weights = [w_out.reshape(n, chans, -1)]
    while len(weights) < m:
        pairs = [(d, d ^ len(weights)) for d in range(m)]
        if len(weights) == 1:
            weights.append(lax.ppermute(weights[0], "ch", pairs))
        else:
            for even in list(weights[::2]):
                far = lax.ppermute(even, "ch", pairs)
                weights += [far, lax.ppermute(far, "ch", [(d, d ^ 1) for d in range(m)])]

    packed = pack(outer_gate, inner_gate, values_in, filters, n)
    packed = lax.all_to_all(packed, "ctx", 0, 0)
    skip = lax.dynamic_slice_in_dim(skip_gain, j * chans, chans, 0)[None, :]
    packed, weights = lax.optimization_barrier((packed, weights))
    parts = list(convolve(here, packed, skip, places))
    parts = parts[:1] + [
        lax.ppermute(part, "ch", [(d, d ^ b) for d in range(m)]) for b, part in enumerate(parts) if b
    ]

    ring = ring_of(4, across)
    spot = np.argsort(np.array(ring))
    routes = [[(ring[p], ring[(p + way) % n]) for p in range(n)] for way in (1, -1)]

    def owners(*offsets):
        return np.array([[ring[(spot[a] + o) % n] for o in offsets] for a in range(n)], np.int32)

    own = [jnp.stack(parts[:half]), jnp.stack(parts[half:])]
    tips = [[piece, piece] for piece in own]
    arrived, sums = [([own], [0])], None
    for s in range(1, n // 2 + 1):
        if s >= 3:
            ready = arrived[: s - 1] if s == 3 else arrived[s - 2 : s - 1]
            pieces, offsets = (sum(lists, []) for lists in zip(*ready))
            sums = project(pieces, owners(*offsets), sums, here, weights)
            tips[0], sums = lax.optimization_barrier((tips[0], sums))
        for h in range(2):
            for way in range(2) if s < n // 2 else [h]:
                tips[h][way] = lax.ppermute(tips[h][way], "ctx", routes[way])
        if s < n // 2:
            arrived.append(([list(piece) for piece in zip(*tips)], [-s, s]))
    pieces, offsets = arrived[-1]
    sums = project(pieces, owners(*offsets), sums, here, weights, grant=51)
    final = [[tips[0][0], tips[1][1]]]
    sent = project(final, owners(n // 2), sums, here, weights, last=True, grant=51)

    found = []
    for e in range(2):
        route = []
        for a in range(n):
            for b in range(m):
                route.append((a * m + b, row_block((a + e) % 2, b) * m + a // 2))
        found.append(lax.ppermute(sent[e], ("ctx", "ch"), route))
    even = (j // across) % 2 == 0
    return jnp.where(even, jnp.concatenate(found, axis=1), jnp.concatenate(found[::-1], axis=1))


def solution(mesh):
    placed = (
        P("ctx", "ch"),
        P("ctx", "ch"),
        P("ctx", "ch"),
        P("ctx", "ch"),
        P("ch"),
        P("ch", "ctx"),
    )
    return jax.shard_map(
        per_device, mesh=mesh, in_specs=placed, out_specs=P("ctx", "ch"), check_vma=False
    )
```
